256 devices in a mesh: ep: 16 (over y, z_lo), dp: 16 (over x, z_hi, core).
Axes of the slice: x: 4, y: 4, z: 8 (z_hi: 2, z_lo: 4; z = z_hi * 4 + z_lo), core: 2. Of those that a mesh axis runs over, the one named last changes fastest.
Arguments:
- tokens: bfloat16 [32768, 2048], P(('ep', 'dp')), may hold values from -6 to 6
- grad_out: bfloat16 [32768, 2048], P(('ep', 'dp')), may hold values from -6 to 6
- routes: int32 [32768, 8], P(('ep', 'dp')), may hold values from 0 to 31, all different within a row; in each aligned block of 128 rows (0 to 127, 128 to 255, ...) at most 40 rows name the same one
- probs: float32 [32768, 8], P(('ep', 'dp')), may hold values from 0.02 to 0.3
- old_place: int32 [32], replicated, may hold values from 0 to 31, as said below
- new_place: int32 [32], replicated, may hold values from 0 to 31, as said below
- gate_w: bfloat16 [32, 2048, 512], P('ep', 'dp'), may hold values from -0.125 to 0.125
- gate_m: bfloat16 [32, 2048, 512], P('ep', 'dp'), may hold values from -6 to 6
- gate_v: bfloat16 [32, 2048, 512], P('ep', 'dp'), may hold values from 0.5 to 8
- down_w: bfloat16 [32, 512, 2048], P('ep', None, 'dp'), may hold values from -0.25 to 0.25
- down_m: bfloat16 [32, 512, 2048], P('ep', None, 'dp'), may hold values from -6 to 6
- down_v: bfloat16 [32, 512, 2048], P('ep', None, 'dp'), may hold values from 0.5 to 8
Outputs:
- mixed: bfloat16 [32768, 2048], P(('ep', 'dp'))
- grad_tokens: bfloat16 [32768, 2048], P(('ep', 'dp'))
- grad_probs: float32 [32768, 8], P(('ep', 'dp'))
- gate_w_next: bfloat16 [32, 2048, 512], P('ep', 'dp')
- gate_m_next: bfloat16 [32, 2048, 512], P('ep', 'dp')
- gate_v_next: bfloat16 [32, 2048, 512], P('ep', 'dp')
- down_w_next: bfloat16 [32, 512, 2048], P('ep', None, 'dp')
- down_m_next: bfloat16 [32, 512, 2048], P('ep', None, 'dp')
- down_v_next: bfloat16 [32, 512, 2048], P('ep', None, 'dp')
The draws below stay inside these ranges and needn't reach their ends.
Inputs may be any that keep to these rules, and one draw needn't show every extreme that they name: `old_place`: A permutation of the experts; slot s lies on ep rank s // 2. `new_place`: equal to old_place except in exactly 3 slots, one on each of the ep ranks r, r - 1 and r - 1 - 16 // 2 (modulo 16) for some r; the slot on rank r receives the expert of the slot on r - 1, that one the expert of the slot on r - 1 - 16 // 2, and that one the expert of the slot on r. `routes`: A row's 8 experts differ; in each aligned block of 128 rows (the rows of one device) no expert is named by more than 40 rows, and in some block one expert is named by exactly 40 rows.
All inputs are finite; a program needn't handle non-finite values.
Results may differ from the reference program's by a relative error of at most 0.025.
Values may be sent and summed in bfloat16 or wider, within the bound.
No kernel may reach another device: no remote copies, remote signals or barrier semaphores. Data moves between devices by JAX's collectives and lax.ppermute only.
A program may use at most 128 MiB of HBM per device.

```python
import math
import jax
import jax.numpy as jnp
import numpy as np
from jax import lax

D = 2048
FF = 512
EXPERTS = 32
TOP = 8
TOK_DEV = 128
MOVES = 3
MOST = 40
TOKENS = 32768
N_EP = 16
N_DP = 16


def placement_pair(key):
    local_count = EXPERTS // N_EP
    old_slots = jax.random.permutation(key, EXPERTS).astype(jnp.int32)
    first_rank = jax.random.randint(jax.random.fold_in(key, 11), (), 0, N_EP).astype(jnp.int32)
    ranks = jnp.stack([first_rank, (first_rank - 1) % N_EP, (first_rank - 1 - N_EP // 2) % N_EP]).astype(jnp.int32)
    offsets = jax.random.randint(jax.random.fold_in(key, 12), (MOVES,), 0, local_count).astype(jnp.int32)
    chosen = ranks * local_count + offsets
    new_slots = old_slots.at[chosen].set(old_slots[jnp.roll(chosen, -1)])
    return (old_slots, new_slots)


def draw_old_place(key, part):
    placed = placement_pair(key)
    return placed[0]


def draw_new_place(key, part):
    placed = placement_pair(key)
    return placed[1]


def block_levels(own_key, dims, cuts, low, largest):
    loudness = 1.0
    for dim, blocks in cuts:
        steps = jax.random.uniform(jax.random.fold_in(jax.random.fold_in(own_key, 6), dim), (blocks,), jnp.float32, low / len(cuts), largest / len(cuts))
        loudness = loudness * jnp.repeat(jnp.exp(steps), dims[dim] // blocks).reshape((-1,) + (1,) * (len(dims) - 1 - dim))
    return loudness


def deal_out(rng, own, number, rows, number_of, top, most, skew):
    order = jax.random.permutation(rng, number_of)
    packed, usual = load_shares(number_of, rows * top, most, skew, True), load_shares(number_of, rows * top, most, skew, False)
    places = jnp.arange(number_of)

    def named(lengths, offset_by):
        used = int((lengths > 0).sum())
        fixed = max(1, used // 4)
        moved = fixed + (places - fixed + offset_by * (used - fixed)) % max(1, number_of - fixed)
        return jnp.zeros((number_of,), jnp.int32).at[order[jnp.where(places < fixed, places, moved)]].set(jnp.asarray(lengths, jnp.int32))

    lengths = jnp.where(number % 4 == 0, named(packed, number // 4), named(usual, number - number // 4 - 1))
    mixed = jax.random.permutation(jax.random.fold_in(own, 3), number_of)
    giver, taker = mixed[0:number_of // 2 * 2:2], mixed[1:number_of // 2 * 2:2]
    room = jnp.minimum(lengths[giver] - 1, most - lengths[taker]) // 2
    room = jnp.where((giver == order[0]) | (taker == order[0]) | (lengths[taker] == 0), 0, jnp.maximum(room, 0))
    moved = jax.random.randint(jax.random.fold_in(own, 4), (number_of // 2,), 0, 1 << 20) % (room + 1)
    lengths = lengths.at[giver].add(-moved).at[taker].add(moved)
    items = jnp.searchsorted(jnp.cumsum(lengths), jnp.arange(rows * top), side="right").astype(jnp.int32)
    listing = items.reshape(top, rows).T
    listing = listing[jax.random.permutation(jax.random.fold_in(own, 1), rows)]
    offset_by = jax.random.randint(jax.random.fold_in(own, 2), (rows, 1), 0, top)
    return jnp.take_along_axis(listing, (jnp.arange(top)[None, :] + offset_by) % top, axis=1)


def load_shares(count, total, reach, lean, full):
    loads = [(1 << 20) // math.isqrt(grade ** lean) + 1 for grade in range(1, count + 1)]
    largest = reach if full else min(reach, max(-(-total // count), total * loads[0] // sum(loads)))
    least = 1 if total - largest >= count - 1 else 0
    given, spare = [largest] + [least] * (count - 1), total - largest - least * (count - 1)
    while spare > 0:
        free = [i for i in range(1, count) if given[i] < largest] or [i for i in range(1, count) if given[i] < reach]
        mass, budget = sum([loads[i] for i in free]), spare
        for i in free:
            extra = min(reach - given[i], max(1, budget * loads[i] // mass), spare)
            given[i] = given[i] + extra
            spare = spare - extra
    return np.array(given)


def scatter_about(own_key, extent, width, bound, cuts=(), kind=jnp.bfloat16):
    gain = block_levels(own_key, extent, cuts, -0.22, 0.18) if cuts else 1.0
    drawn = jax.random.normal(own_key, extent, jnp.float32) * width * gain
    return jnp.minimum(jnp.maximum(drawn, -bound), bound).astype(kind)


def setup_inputs(seed: int = 0) -> dict:
    splits = jax.random.split(jax.random.key(seed), 13)
    tokens = scatter_about(splits[0], (TOKENS, D), 1.0, 6.0, ((0, 256),))
    grad_out = scatter_about(splits[1], (TOKENS, D), 1.0, 6.0, ((0, 256),))
    routes_keys = jax.random.split(jax.random.fold_in(splits[2], 1), TOKENS // TOK_DEV)
    routes_turns = jax.random.permutation(jax.random.fold_in(splits[2], 3), TOKENS // TOK_DEV)
    routes = jax.vmap(lambda own, number: deal_out(jax.random.fold_in(splits[2], 2), own, number, TOK_DEV, EXPERTS, TOP, MOST, 2))(routes_keys, routes_turns).reshape((TOKENS, TOP))
    probs = jnp.clip(0.02 + 0.28 * jax.random.uniform(splits[3], (TOKENS, TOP), jnp.float32) ** block_levels(splits[3], (TOKENS, TOP), ((0, 256),), -0.2, 0.2), 0.02, 0.3)
    old_place = draw_old_place(jax.random.fold_in(splits[12], 71), 0)
    new_place = draw_new_place(jax.random.fold_in(splits[12], 71), 0)
    gate_w = scatter_about(splits[6], (EXPERTS, D, FF), D ** -0.5, 0.125, ((0, 16), (1, 16)))
    gate_m = scatter_about(splits[7], (EXPERTS, D, FF), 1.0, 6.0, ((0, 16), (1, 16)))
    gate_v = jnp.clip(jnp.exp(math.log(8.0) - 2.7725887 * jax.random.uniform(splits[8], (EXPERTS, D, FF), jnp.float32) ** block_levels(splits[8], (EXPERTS, D, FF), ((0, 16), (1, 16)), -0.2, 0.2)), 0.5, 8.0).astype(jnp.bfloat16)
    down_w = scatter_about(splits[9], (EXPERTS, FF, D), FF ** -0.5, 0.25, ((0, 16), (2, 16)))
    down_m = scatter_about(splits[10], (EXPERTS, FF, D), 1.0, 6.0, ((0, 16), (2, 16)))
    down_v = jnp.clip(jnp.exp(math.log(8.0) - 2.7725887 * jax.random.uniform(splits[11], (EXPERTS, FF, D), jnp.float32) ** block_levels(splits[11], (EXPERTS, FF, D), ((0, 16), (2, 16)), -0.2, 0.2)), 0.5, 8.0).astype(jnp.bfloat16)
    return dict(tokens=tokens, grad_out=grad_out, routes=routes, probs=probs, old_place=old_place, new_place=new_place, gate_w=gate_w, gate_m=gate_m, gate_v=gate_v, down_w=down_w, down_m=down_m, down_v=down_v)


beta_one = 0.9
beta_two = 0.95
step_rate = 0.001
adam_eps = 1e-08

def silu_slope(values):
    sigmoid = jax.nn.sigmoid(values)
    return sigmoid * (1.0 + values * (1.0 - sigmoid))

def expert_pass(operands):
    inputs, upstream, gate_full, down_full = operands
    pre = jnp.dot(inputs, gate_full, preferred_element_type=jnp.float32)
    hidden = jax.nn.silu(pre).astype(jnp.bfloat16)
    outputs = jnp.dot(hidden, down_full, preferred_element_type=jnp.float32).astype(jnp.bfloat16)
    contract_last = (((1,), (1,)), ((), ()))
    contract_first = (((0,), (0,)), ((), ()))
    d_hidden = lax.dot_general(upstream, down_full, contract_last, preferred_element_type=jnp.float32)
    d_pre = (d_hidden * silu_slope(pre)).astype(jnp.bfloat16)
    d_inputs = lax.dot_general(d_pre, gate_full, contract_last, preferred_element_type=jnp.float32).astype(jnp.bfloat16)
    gate_part = lax.dot_general(inputs, d_pre, contract_first, preferred_element_type=jnp.float32).astype(jnp.bfloat16)
    down_part = lax.dot_general(hidden, upstream, contract_first, preferred_element_type=jnp.float32).astype(jnp.bfloat16)
    return (outputs, d_inputs, gate_part, down_part)

def adam_update(weight, first, second, grad):
    first_new = beta_one * first.astype(jnp.float32) + (1.0 - beta_one) * grad
    second_new = beta_two * second.astype(jnp.float32) + (1.0 - beta_two) * grad * grad
    weight_new = weight.astype(jnp.float32) - step_rate * first_new / (jnp.sqrt(second_new) + adam_eps)
    return (weight_new.astype(jnp.bfloat16), first_new.astype(jnp.bfloat16), second_new.astype(jnp.bfloat16))

def reference(tokens, grad_out, routes, probs, old_place, new_place, gate_w, gate_m, gate_v, down_w, down_m, down_v):
    slots = jnp.arange(EXPERTS, dtype=jnp.int32)
    inverse_old = lax.optimization_barrier(jnp.sum(jnp.where(old_place[None, :] == slots[:, None], slots[None, :], 0), axis=1)).astype(jnp.int32)
    gate_expert = gate_w[inverse_old]
    down_expert = down_w[inverse_old]
    grouped_tokens = tokens.reshape(N_EP, N_DP, TOK_DEV, D)
    grouped_grads = grad_out.reshape(N_EP, N_DP, TOK_DEV, D)
    grouped_routes = routes.reshape(N_EP, N_DP, TOK_DEV * TOP)
    grouped_probs = probs.reshape(N_EP, N_DP, TOK_DEV, TOP)
    sources = jnp.arange(N_EP, dtype=jnp.int32)

    def per_index(carry, index):
        gate_total, down_total = carry
        local_tokens = lax.dynamic_index_in_dim(grouped_tokens, index, 1, keepdims=False)
        local_grads = lax.dynamic_index_in_dim(grouped_grads, index, 1, keepdims=False)
        route_ids = lax.dynamic_index_in_dim(grouped_routes, index, 1, keepdims=False)
        local_probs = lax.dynamic_index_in_dim(grouped_probs, index, 1, keepdims=False)
        hits = (route_ids[:, :, None] == slots[None, None, :]).astype(jnp.int32)
        within = lax.optimization_barrier(jnp.sum((jnp.cumsum(hits, axis=1) - 1) * hits, axis=2)).astype(jnp.int32)
        row_index = (sources[:, None] * MOST + within).astype(jnp.int32)
        copies = jnp.repeat(local_tokens, TOP, axis=1)
        scaled = (local_probs[:, :, :, None] * local_grads[:, :, None, :].astype(jnp.float32)).astype(jnp.bfloat16)
        scaled = scaled.reshape(N_EP, TOK_DEV * TOP, D)
        inputs = jnp.zeros((EXPERTS, N_EP * MOST, D), jnp.bfloat16).at[route_ids, row_index].set(copies)
        upstream = jnp.zeros((EXPERTS, N_EP * MOST, D), jnp.bfloat16).at[route_ids, row_index].set(scaled)
        outputs, d_inputs, gate_part, down_part = lax.map(expert_pass, (inputs, upstream, gate_expert, down_expert))
        out_rows = outputs[route_ids, row_index].astype(jnp.float32).reshape(N_EP, TOK_DEV, TOP, D)
        back_rows = d_inputs[route_ids, row_index].astype(jnp.float32).reshape(N_EP, TOK_DEV, TOP, D)
        mixed_part = lax.optimization_barrier(jnp.sum(local_probs[:, :, :, None] * out_rows, axis=2)).astype(jnp.bfloat16)
        grad_part = lax.optimization_barrier(jnp.sum(back_rows, axis=2)).astype(jnp.bfloat16)
        prob_part = lax.optimization_barrier(jnp.sum(local_grads[:, :, None, :].astype(jnp.float32) * out_rows, axis=3))
        carry = (gate_total + gate_part.astype(jnp.float32), down_total + down_part.astype(jnp.float32))
        return (carry, (mixed_part, grad_part, prob_part))
    start = (jnp.zeros((EXPERTS, D, FF), jnp.float32), jnp.zeros((EXPERTS, FF, D), jnp.float32))
    totals, pieces = lax.scan(per_index, start, jnp.arange(N_DP, dtype=jnp.int32))
    gate_grad, down_grad = totals
    mixed = jnp.transpose(pieces[0], (1, 0, 2, 3)).reshape(TOKENS, D)
    grad_tokens = jnp.transpose(pieces[1], (1, 0, 2, 3)).reshape(TOKENS, D)
    grad_probs = jnp.transpose(pieces[2], (1, 0, 2, 3)).reshape(TOKENS, TOP)
    source_slots = inverse_old[new_place]
    gate_next = adam_update(gate_w[source_slots], gate_m[source_slots], gate_v[source_slots], gate_grad[new_place])
    down_next = adam_update(down_w[source_slots], down_m[source_slots], down_v[source_slots], down_grad[new_place])
    return (mixed, grad_tokens, grad_probs, gate_next[0], gate_next[1], gate_next[2], down_next[0], down_next[1], down_next[2])
```

```python
import jax
import jax.numpy as jnp
from jax import lax
from jax.sharding import PartitionSpec as P

beta_one = 0.9
beta_two = 0.95
step_rate = 0.001
adam_eps = 1e-08

BOTH = ("ep", "dp")
N_Y, N_ZL, N_X, N_ZH, N_C = 4, 4, 4, 2, 2
N_EP, N_DP = N_Y * N_ZL, N_X * N_ZH * N_C
F32, BF16 = jnp.float32, jnp.bfloat16


def links(move):
    pairs = []
    for ep in range(N_EP):
        for dp in range(N_DP):
            y, zl = divmod(ep, N_ZL)
            x, rest = divmod(dp, N_ZH * N_C)
            zh, c = divmod(rest, N_C)
            y, x, z, c = move(y, x, zh * N_ZL + zl, c)
            zh, zl = divmod(z % (N_ZH * N_ZL), N_ZL)
            there = (y % N_Y * N_ZL + zl) * N_DP + x % N_X * N_ZH * N_C + zh * N_C + c
            pairs.append((ep * N_DP + dp, there))
    return pairs


Y_UP = links(lambda y, x, z, c: (y + 1, x, z, c))
Y_DOWN = links(lambda y, x, z, c: (y - 1, x, z, c))
X_UP = links(lambda y, x, z, c: (y, x + 1, z, c))
X_DOWN = links(lambda y, x, z, c: (y, x - 1, z, c))
Z_UP = links(lambda y, x, z, c: (y, x, z + 2, c))
Z_DOWN = links(lambda y, x, z, c: (y, x, z - 2, c))
Z_PAIR = links(lambda y, x, z, c: (y, x, z ^ 1, c))
CORE = links(lambda y, x, z, c: (y, x, z, 1 - c))


def send(block, pairs):
    return lax.ppermute(block, BOTH, pairs)


def spread(block, up, down):
    half = block.shape[0] // 2
    left, right = send(block, up), send(block, down)
    far = [send(left[:half], up), send(right[half:], down)]
    return [block, left, right] + far


def collect(blocks, up, down):
    own, left, right, far = blocks
    half = far.shape[0] // 2
    from_left, from_right = send(far[:half], up), send(far[half:], down)
    right = jnp.concatenate([add(right[:half], from_left), right[half:]], axis=0)
    left = jnp.concatenate([left[:half], add(left[half:], from_right)], axis=0)
    return own, send(right, up), send(left, down)


def add(first, second):
    return (first.astype(F32) + second.astype(F32)).astype(BF16)


def choose(index, options):
    picked = options[0]
    for number in range(1, len(options)):
        picked = jnp.where(index == number, options[number], picked)
    return picked


def to_relative(rows, x, zh, c):
    width = rows.shape[1] // N_DP
    part = lambda i, j, k: rows[:, ((i * N_ZH + j) * N_C + k) * width :][:, :width]
    cols = []
    for j in range(N_ZH):
        for k in range(N_C):
            for step in (0, -1, 1, 2):
                by_x = []
                for i in range(N_X):
                    source = (i + step) % N_X
                    by_x.append(
                        choose(zh * N_C + c, [part(source, j ^ (n // N_C), k ^ (n % N_C)) for n in range(4)])
                    )
                cols.append(choose(x, by_x))
    return jnp.concatenate(cols, axis=1)


def to_absolute(rows, x, zh, c):
    width = rows.shape[1] // N_DP
    place = {0: 0, 3: 1, 1: 2, 2: 3}
    part = lambda j, k, step: rows[:, ((j * N_C + k) * N_X + place[step % N_X]) * width :][:, :width]
    cols = []
    for i in range(N_X):
        for j in range(N_ZH):
            for k in range(N_C):
                by_x = [
                    choose(zh * N_C + c, [part(j ^ (n // N_C), k ^ (n % N_C), i - here) for n in range(4)])
                    for here in range(N_X)
                ]
                cols.append(choose(x, by_x))
    return jnp.concatenate(cols, axis=1)


def adam_update(weight, first, second, grad):
    first_new = beta_one * first.astype(F32) + (1.0 - beta_one) * grad
    second_new = beta_two * second.astype(F32) + (1.0 - beta_two) * grad * grad
    weight_new = weight.astype(F32) - step_rate * first_new / (jnp.sqrt(second_new) + adam_eps)
    return weight_new.astype(BF16), first_new.astype(BF16), second_new.astype(BF16)


def dot(left, right, dims=((1,), (0,))):
    return lax.dot_general(left, right, (dims, ((), ())), preferred_element_type=F32)


ROWS = ((0,), (0,))
COLS = ((1,), (1,))


def per_device(tokens, grad_out, routes, probs, old_place, new_place, gate_w, gate_m, gate_v, down_w, down_m, down_v):
    tok_rows, width = tokens.shape
    choose_count = routes.shape[1]
    experts = old_place.shape[0]
    local_count, shard, hidden = gate_w.shape
    ep, dp = lax.axis_index("ep"), lax.axis_index("dp")
    y, zl = ep // N_ZL, ep % N_ZL
    zb, za = zl // 2, zl % 2
    x, zh, c = dp // (N_ZH * N_C), dp // N_C % N_ZH, dp % N_C
    slots = jnp.arange(experts, dtype=jnp.int32)

    changed = new_place != old_place
    source = jnp.sum(jnp.where(new_place[:, None] == old_place[None, :], slots[None, :], 0), axis=1)
    first = changed & (source // local_count == (slots // local_count - 1) % N_EP)
    root = jnp.sum(jnp.where(first, slots // local_count, 0))
    mine = lax.dynamic_slice_in_dim(changed, ep * local_count, local_count)
    moved = mine[1:].astype(jnp.int32).sum()

    def side(state):
        return jnp.transpose(state, (0, 2, 1))

    def migrate(payload):
        def branch(rank):
            stops = [(rank - 1) % N_EP, rank, (rank - 1 - N_EP // 2) % N_EP, (rank - 1) % N_EP]
            pairs = [(stops[0], stops[1]), (stops[2], stops[3]), (stops[1], stops[2])]
            return lambda block: lax.ppermute(block, "ep", pairs)

        return lax.switch(root, [branch(rank) for rank in range(N_EP)], payload)

    def settle(states, arrived):
        out = []
        for number, state in enumerate(states):
            fresh = arrived[:, number * hidden : (number + 1) * hidden]
            out.append([jnp.where(mine[n], fresh, state[n]) for n in range(local_count)])
        return out

    def payload_of(states):
        return jnp.concatenate([jnp.where(moved == 1, state[1], state[0]) for state in states], axis=1)

    weights = [gate_w, side(down_w)]
    moments = [gate_m, gate_v, side(down_m), side(down_v)]
    gate_now, down_now = settle(weights, migrate(payload_of(weights)))
    block = jnp.concatenate(gate_now + down_now, axis=1)

    half = shard // 2
    z_left, z_right = send(block, Z_UP), send(block, Z_DOWN)
    far = jnp.concatenate([send(z_left[:half], Z_UP), send(z_right[half:], Z_DOWN)], axis=0)
    near = [jnp.where(zb == 1, z_left, z_right), jnp.where(zb == 1, z_right, z_left)]

    def gather_x(piece):
        own = jnp.concatenate(spread(piece, X_UP, X_DOWN), axis=0)
        return [own, send(own, CORE)]

    own_parts = gather_x(block)
    near_parts = gather_x(near[0]) + gather_x(near[1])
    own_parts = own_parts + gather_x(far)
    cut = local_count * hidden
    gate_full = [jnp.concatenate([p[:, :cut] for p in parts], axis=0) for parts in (own_parts, near_parts)]
    down_full = [jnp.concatenate([p[:, cut:] for p in parts], axis=0) for parts in (own_parts, near_parts)]

    tokens_here = to_relative(tokens, x, zh, c)
    grads_here = to_relative(grad_out, x, zh, c)
    tokens_pair, grads_pair = send(tokens_here, Z_PAIR), send(grads_here, Z_PAIR)

    def gather_y(piece):
        return jnp.concatenate(spread(piece, Y_UP, Y_DOWN), axis=0)

    tok = [gather_y(tokens_here), gather_y(tokens_pair)]
    grd = [gather_y(grads_here), gather_y(grads_pair)]

    inverse_new = jnp.sum(jnp.where(new_place[None, :] == slots[:, None], slots[None, :], 0), axis=1)
    new_slot = jnp.sum(jnp.where(routes[:, :, None] == slots, inverse_new, 0), axis=2)
    hits = new_slot[:, :, None] == slots
    by_slot = jnp.sum(jnp.where(hits, probs[:, :, None], 0.0), axis=1)
    all_probs = lax.all_gather(by_slot, "ep", axis=0)
    spans = []
    for other in (0, 1):
        zl_there = (zb ^ other) * 2 + za
        spans.append((y * N_ZL + zl_there) * local_count)
    own_probs = []
    for pair in (0, 1):
        rows = []
        for step in (0, -1, 1, 2):
            rank = (y + step) % N_Y * N_ZL + zb * 2 + (za ^ pair)
            rows.append(lax.dynamic_index_in_dim(all_probs, rank, 0, keepdims=False))
        rows = jnp.concatenate(rows, axis=0)
        own_probs.append([lax.dynamic_slice_in_dim(rows, span, local_count, axis=1) for span in spans])

    def wide(table):
        return jnp.concatenate(
            [jnp.broadcast_to(table[:, n : n + 1], (table.shape[0], hidden)) for n in range(local_count)], axis=1
        )

    weighted, slopes, dots = {}, {}, {}
    for pair in (0, 1):
        for who in (1, 0):
            pre = dot(tok[pair], gate_full[who])
            up = dot(grd[pair], down_full[who])
            scale = wide(own_probs[pair][who])
            sigmoid = jax.nn.sigmoid(pre)
            act = (pre * sigmoid).astype(BF16).astype(F32)
            weighted[pair, who] = (scale * act).astype(BF16)
            slopes[pair, who] = (scale * up * sigmoid * (1.0 + pre * (1.0 - sigmoid))).astype(BF16)
            dots[pair, who] = [
                jnp.sum((act * up)[:, n * hidden : (n + 1) * hidden], axis=1) for n in range(local_count)
            ]

    def scatter_y(rows):
        blocks = [rows[n * tok_rows : (n + 1) * tok_rows] for n in range(4)]
        own, left, right = collect(blocks, Y_UP, Y_DOWN)
        return own.astype(F32) + left.astype(F32) + right.astype(F32)

    mixed, back = [], []
    for pair in (0, 1):
        rows = dot(weighted[pair, 0], down_full[0], COLS) + dot(weighted[pair, 1], down_full[1], COLS)
        mixed.append(scatter_y(rows.astype(BF16)))
        rows = dot(slopes[pair, 0], gate_full[0], COLS) + dot(slopes[pair, 1], gate_full[1], COLS)
        back.append(scatter_y(rows.astype(BF16)))
    mixed = mixed[0] + send(mixed[1].astype(BF16), Z_PAIR).astype(F32)
    back = back[0] + send(back[1].astype(BF16), Z_PAIR).astype(F32)
    mixed = to_absolute(mixed.astype(BF16), x, zh, c)
    grad_tokens = to_absolute(back.astype(BF16), x, zh, c)

    table = jnp.zeros((N_EP, 2 * local_count, tok_rows), F32)
    for pair in (0, 1):
        entry = jnp.stack(dots[pair, 0] + dots[pair, 1], axis=0)
        for number, step in enumerate((0, -1, 1, 2)):
            rank = (y + step) % N_Y * N_ZL + zb * 2 + (za ^ pair)
            piece = entry[:, number * tok_rows : (number + 1) * tok_rows]
            table = lax.dynamic_update_slice_in_dim(table, piece[None], rank, 0)
    table = lax.all_to_all(table, "ep", split_axis=0, concat_axis=0, tiled=True)
    table = table.reshape(N_Y, 2, 2, 2, local_count, tok_rows)
    table = jnp.where(zb == 1, table[:, 1], table[:, 0])
    table = jnp.where(zb == 1, table[:, :, ::-1], table)
    table = jnp.transpose(table, (0, 2, 1, 3, 4)).reshape(experts, tok_rows)
    grad_probs = jnp.sum(jnp.where(hits, jnp.transpose(table)[:, None, :], 0.0), axis=2)

    def scatter_x(who):
        gate = dot(tok[0], slopes[0, who], ROWS) + dot(tok[1], slopes[1, who], ROWS)
        down = dot(grd[0], weighted[0, who], ROWS) + dot(grd[1], weighted[1, who], ROWS)
        part = jnp.concatenate([gate, down], axis=1).astype(BF16)
        rows = N_X * shard
        out = []
        for n in range(N_ZH):
            ours = part[2 * n * rows : (2 * n + 1) * rows]
            theirs = part[(2 * n + 1) * rows : (2 * n + 2) * rows]
            total = add(ours, send(theirs, CORE))
            own, left, right = collect([total[i * shard : (i + 1) * shard] for i in range(4)], X_UP, X_DOWN)
            out.append(own.astype(F32) + left.astype(F32) + right.astype(F32))
        return out

    near_grads = scatter_x(1)
    own_grads = scatter_x(0)
    to_right = jnp.where(zb == 1, near_grads[1], near_grads[0])
    to_left = jnp.where(zb == 1, near_grads[0], near_grads[1])
    distant = own_grads[1].astype(BF16)
    from_left, from_right = send(distant[:half], Z_UP), send(distant[half:], Z_DOWN)
    to_right = jnp.concatenate([to_right[:half] + from_left.astype(F32), to_right[half:]], axis=0).astype(BF16)
    to_left = jnp.concatenate([to_left[:half], to_left[half:] + from_right.astype(F32)], axis=0).astype(BF16)
    grad = own_grads[0] + send(to_right, Z_UP).astype(F32) + send(to_left, Z_DOWN).astype(F32)

    gate_m_now, gate_v_now, down_m_now, down_v_now = settle(moments, migrate(payload_of(moments)))
    gate_next, down_next = [], []
    for n in range(local_count):
        piece = grad[:, n * hidden : (n + 1) * hidden]
        gate_next.append(adam_update(gate_now[n], gate_m_now[n], gate_v_now[n], piece))
        piece = grad[:, (local_count + n) * hidden : (local_count + n + 1) * hidden]
        done = adam_update(down_now[n], down_m_now[n], down_v_now[n], piece)
        down_next.append([jnp.transpose(entry) for entry in done])
    stacked = [jnp.stack([entry[i] for entry in gate_next], axis=0) for i in range(3)]
    stacked += [jnp.stack([entry[i] for entry in down_next], axis=0) for i in range(3)]
    return (mixed, grad_tokens, grad_probs, *stacked)


def solution(mesh):
    tok = P(("ep", "dp"), None)
    gate, down = P("ep", "dp", None), P("ep", None, "dp")
    in_specs = (tok, tok, tok, tok, P(), P(), gate, gate, gate, down, down, down)
    out_specs = (tok, tok, tok, gate, gate, gate, down, down, down)
    return jax.shard_map(per_device, mesh=mesh, in_specs=in_specs, out_specs=out_specs, check_vma=False)
```

```python
import functools
import jax
import jax.numpy as jnp
from jax import lax
from jax.experimental import pallas as pl
from jax.experimental.pallas import tpu as pltpu
from jax.sharding import PartitionSpec as P

beta_one = 0.9
beta_two = 0.95
step_rate = 0.001
adam_eps = 1e-08

BOTH = ("ep", "dp")
N_Y, N_ZL, N_X, N_ZH, N_C = 4, 4, 4, 2, 2
N_EP, N_DP = N_Y * N_ZL, N_X * N_ZH * N_C
F32, BF16 = jnp.float32, jnp.bfloat16


def links(move):
    pairs = []
    for ep in range(N_EP):
        for dp in range(N_DP):
            y, zl = divmod(ep, N_ZL)
            x, rest = divmod(dp, N_ZH * N_C)
            zh, c = divmod(rest, N_C)
            y, x, z, c = move(y, x, zh * N_ZL + zl, c)
            zh, zl = divmod(z % (N_ZH * N_ZL), N_ZL)
            there = (y % N_Y * N_ZL + zl) * N_DP + x % N_X * N_ZH * N_C + zh * N_C + c
            pairs.append((ep * N_DP + dp, there))
    return pairs


Y_UP = links(lambda y, x, z, c: (y + 1, x, z, c))
Y_DOWN = links(lambda y, x, z, c: (y - 1, x, z, c))
X_UP = links(lambda y, x, z, c: (y, x + 1, z, c))
X_DOWN = links(lambda y, x, z, c: (y, x - 1, z, c))
Z_UP = links(lambda y, x, z, c: (y, x, z + 2, c))
Z_DOWN = links(lambda y, x, z, c: (y, x, z - 2, c))
Z_PAIR = links(lambda y, x, z, c: (y, x, z ^ 1, c))
Z_FAR = links(lambda y, x, z, c: (y, x, z + 4, c))
X_GROUPS = [[i * N_ZH * N_C + rest for i in range(N_X)] for rest in range(N_ZH * N_C)]
ROOM = 48
EXTRA = 16
VMEM = 56 * 2**20
SCALE = 100
CORE = links(lambda y, x, z, c: (y, x, z, 1 - c))


E_NEXT = [(rank, (rank + 1) % N_EP) for rank in range(N_EP)]
E_HALF = [(rank, (rank + N_EP // 2) % N_EP) for rank in range(N_EP)]
E_BACK = [(rank, (rank - 1 - N_EP // 2) % N_EP) for rank in range(N_EP)]


def after(array, *others):
    return lax.optimization_barrier((array, *others))[0]


def send(block, pairs):
    return lax.ppermute(block, BOTH, pairs)


def send_ep(block, pairs):
    return lax.ppermute(block, "ep", pairs)


def add(first, second):
    return (first.astype(F32) + second.astype(F32)).astype(BF16)


def adam_update(weight, first, second, grad):
    first_new = beta_one * first.astype(F32) + (1.0 - beta_one) * grad
    second_new = beta_two * second.astype(F32) + (1.0 - beta_two) * grad * grad
    weight_new = weight.astype(F32) - step_rate * first_new / (jnp.sqrt(second_new) + adam_eps)
    return weight_new.astype(BF16), first_new.astype(BF16), second_new.astype(BF16)


def updates(mine, grad, moved, states, arrived):
    local, shard, hidden = states[0].shape

    def body(mine_ref, grad_ref, moved_ref, *refs):
        ins, arrived_ref, outs = refs[:6], refs[6], refs[7:]
        for n in range(local):
            here = mine_ref[n] > 0
            for side in (0, 1):
                span = slice((side * local + n) * hidden, (side * local + n + 1) * hidden)
                value = jnp.where(here, moved_ref[:, side * hidden : (side + 1) * hidden].astype(F32), grad_ref[:, span])
                if side:
                    value = value.T
                state = []
                for kind in range(3):
                    column = (side * 3 + kind) * hidden
                    fresh = arrived_ref[:, column : column + hidden].astype(F32)
                    old = ins[side * 3 + kind][n].astype(F32)
                    state.append(jnp.where(here, fresh.T if side else fresh, old))
                for kind, done in enumerate(adam_update(*state, value)):
                    outs[side * 3 + kind][n] = done

    shapes = [jax.ShapeDtypeStruct(state.shape, BF16) for state in states]
    moved_bytes = 4 * 6 * local * shard * hidden
    return call(
        body, [SCALARS] + [NEAR] * 9, [(NEAR, shape) for shape in shapes], 0, moved_bytes
    )(mine, grad, moved, *states, arrived)


def dot(left, right, dims=((1,), (0,))):
    return lax.dot_general(left, right, (dims, ((), ())), preferred_element_type=F32)


COLS = ((1,), (1,))
ROWS = ((0,), (0,))
NEAR = pl.BlockSpec(memory_space=pltpu.VMEM)
AWAY = pl.BlockSpec(memory_space=pl.ANY)
SCALARS = pl.BlockSpec(memory_space=pltpu.SMEM)


def call(body, ins, outs, flops, moved, scratch=(), grid=()):
    return pl.pallas_call(
        body,
        grid=grid,
        in_specs=list(ins),
        out_specs=[spec for spec, _ in outs],
        out_shape=[shape for _, shape in outs],
        scratch_shapes=list(scratch),
        compiler_params=pltpu.CompilerParams(vmem_limit_bytes=VMEM),
        cost_estimate=pl.CostEstimate(flops=flops, bytes_accessed=moved, transcendentals=0),
    )


def relative(n, zh, c):
    j, k, i = n // (N_C * N_X), n // N_X % N_C, n % N_X
    return (i * N_ZH + (j ^ zh)) * N_C + (k ^ c)


def pack(place, tokens, grads, table):
    rows, width = tokens.shape
    block = width // N_DP

    def body(place_ref, tok_ref, grd_ref, table_ref, out_ref):
        zh, c = place_ref[0], place_ref[1]
        for n in range(N_DP):
            at = pl.multiple_of(relative(n, zh, c) * block, block)
            here = slice(n * block, (n + 1) * block)
            out_ref[:rows, here] = tok_ref[:, pl.ds(at, block)]
            out_ref[rows : 2 * rows, here] = grd_ref[:, pl.ds(at, block)]
        out_ref[2 * rows :, :] = table_ref[...]

    shape = jax.ShapeDtypeStruct((2 * rows + EXTRA, width), BF16)
    return call(body, [SCALARS] + [NEAR] * 3, [(NEAR, shape)], 0, 8 * rows * width)(place, tokens, grads, table)[0]


def total(place, *arrays):
    rows, width = arrays[0].shape
    rows = (rows - EXTRA) // 2
    block = width // N_DP

    def body(place_ref, *refs):
        zh, c = place_ref[0], place_ref[1]
        ins, (mixed_ref, back_ref, table_ref) = refs[:-3], refs[-3:]

        def added(at, here):
            value = ins[0][at, here].astype(F32)
            for source in ins[1:]:
                value = value + source[at, here].astype(F32)
            return value

        for n in range(N_DP):
            at = pl.multiple_of(relative(n, zh, c) * block, block)
            here = slice(n * block, (n + 1) * block)
            mixed_ref[:, pl.ds(at, block)] = added(slice(0, rows), here).astype(BF16)
            back_ref[:, pl.ds(at, block)] = added(slice(rows, 2 * rows), here).astype(BF16)
        table_ref[...] = added(slice(2 * rows, 2 * rows + EXTRA), slice(0, width))

    outs = [(NEAR, jax.ShapeDtypeStruct((rows, width), BF16))] * 2
    outs.append((NEAR, jax.ShapeDtypeStruct((EXTRA, width), F32)))
    return call(body, [SCALARS] + [NEAR] * len(arrays), outs, 0, 20 * rows * width)(place, *arrays)


def hold(place):
    def body(place_ref, out_ref):
        for n in range(2):
            out_ref[n] = place_ref[n]

    return call(body, [SCALARS], [(SCALARS, jax.ShapeDtypeStruct(place.shape, place.dtype))], 2**40, 0)(place)[0]


def chosen(at, rows):
    return lax.broadcasted_iota(jnp.int32, (rows, at.shape[1]), 0).astype(F32) == at


def inner(blocks, owners, weights, layout, hidden):
    count = len(blocks)
    size, width = blocks[0][0][0].shape[1] // N_DP, blocks[0][0][0].shape[1]
    local = owners.shape[0]
    cut = local * hidden
    rows = count * ROOM
    arrays = []
    for block in blocks:
        for array, _ in block:
            if not any(array is other for other in arrays):
                arrays.append(array)
    index = lambda array: next(n for n, other in enumerate(arrays) if other is array)
    starts = [[(index(array), start) for array, start in block] for block in blocks]
    spans = [(side * local + n) * hidden for n in range(local) for side in (0, 1)]

    def body(owner_ref, *refs):
        sources, stored = refs[: len(arrays)], refs[len(arrays) : len(arrays) + len(weights)]
        x_ref, g_ref, hid_ref, slope_ref, dots_ref, at_ref, held, tables, weight, sem, weight_sem = refs[
            len(arrays) + len(weights) :
        ]
        moves, fills = [], []
        for b, block in enumerate(starts):
            moves.append(
                [
                    pltpu.make_async_copy(
                        sources[which].at[pl.ds(start, size), :],
                        held.at[b, pl.ds(side * size, size), :],
                        sem.at[2 * b + side],
                    )
                    for side, (which, start) in enumerate(block)
                ]
            )
            which, start = block[1]
            moves[b].append(
                pltpu.make_async_copy(
                    sources[which].at[pl.ds(start + size, EXTRA), :], tables.at[b], sem.at[2 * count + b]
                )
            )
        for number, span in enumerate(spans):
            fills.append(
                [
                    pltpu.make_async_copy(
                        stored[which].at[pl.ds(start, depth), pl.ds(span, hidden)],
                        weight.at[pl.ds(to, depth), pl.ds(span, hidden)],
                        weight_sem.at[number * len(layout) + entry],
                    )
                    for entry, (which, start, to, depth) in enumerate(layout)
                ]
            )
        for group in moves + fills:
            for copy in group:
                copy.start()
        factors = [[] for _ in range(local)]
        lines = lax.broadcasted_iota(jnp.int32, (EXTRA, size), 0)
        for b in range(count):
            for copy in moves[b]:
                copy.wait()
            hits = []
            for n in range(local):
                slot = owner_ref[n]
                lanes = pl.ds(pl.multiple_of(slot % N_DP * size, size), size)
                tile = tables[b, :, lanes].astype(F32)
                line = slot // N_DP
                entry = lambda kind: jnp.sum(jnp.where(lines == line + 2 * kind, tile, 0.0), axis=0, keepdims=True)
                number = entry(0)
                at_ref[b * local + n : b * local + n + 1, :] = number
                hits.append(chosen(number, ROOM))
                factors[n].append(jnp.sum(jnp.where(hits[n], entry(1) + entry(2), 0.0), axis=1, keepdims=True))
            pick = jnp.concatenate([hit.astype(F32) for hit in hits], axis=0).astype(BF16)
            for side, target in enumerate((x_ref, g_ref)):
                got = dot(pick, held[b, side * size : (side + 1) * size, :]).astype(BF16)
                for n in range(local):
                    target[n * rows + b * ROOM : n * rows + (b + 1) * ROOM, :] = got[n * ROOM : (n + 1) * ROOM]
        for n in range(local):
            for copy in fills[2 * n] + fills[2 * n + 1]:
                copy.wait()
            mine = slice(n * rows, (n + 1) * rows)
            here = dot(x_ref[mine, :], weight[:, n * hidden : (n + 1) * hidden])
            over = dot(g_ref[mine, :], weight[:, cut + n * hidden : cut + (n + 1) * hidden])
            factor = jnp.concatenate(factors[n], axis=0)
            sigmoid = jax.nn.sigmoid(here)
            act = here * sigmoid
            hid_ref[mine, :] = (factor * act).astype(BF16)
            slope_ref[mine, :] = (factor * over * (sigmoid + act * (1.0 - sigmoid))).astype(BF16)
            sums = jnp.sum(act * over, axis=1, keepdims=True)
            for b in range(count):
                hit = chosen(at_ref[b * local + n : b * local + n + 1, :], ROOM)
                spread = jnp.where(hit, sums[b * ROOM : (b + 1) * ROOM], 0.0)
                dots_ref[b * local + n : b * local + n + 1, :] = jnp.sum(spread, axis=0, keepdims=True)

    shape = lambda last, kind: jax.ShapeDtypeStruct((local * rows, last), kind)
    outs = [(NEAR, shape(width, BF16))] * 2 + [(NEAR, shape(hidden, BF16))] * 2
    outs += [(NEAR, jax.ShapeDtypeStruct((count * local, size), F32))] * 2
    return call(
        body,
        [SCALARS] + [AWAY] * (len(arrays) + len(weights)),
        outs,
        4 * local * rows * width * hidden + 4 * local * ROOM * count * size * width,
        4 * count * size * width + 4 * width * cut + 4 * local * rows * width,
        [
            pltpu.VMEM((count, 2 * size, width), BF16),
            pltpu.VMEM((count, EXTRA, width), BF16),
            pltpu.VMEM((width, 2 * cut), BF16),
            pltpu.SemaphoreType.DMA((3 * count,)),
            pltpu.SemaphoreType.DMA((len(spans) * len(layout),)),
        ],
    )(owners, *arrays, *weights)


def outer(owners, ats, hids, slopes, dots, weights, layouts, part, parts):
    ranks = len(hids)
    size = ats[0].shape[1]
    local = owners.shape[0] // ranks
    hidden = hids[0].shape[1]
    cut = local * hidden
    every = hids[0].shape[0] // local
    rows = every // parts
    blocks = rows // ROOM
    width = size * N_DP
    steps = N_ZH * N_C
    depth = width // steps
    counts = [len(some) for some in weights]
    tall = 2 * size + EXTRA

    def body(owner_ref, *refs):
        at_refs, refs = refs[:ranks], refs[ranks:]
        hid_refs, refs = refs[:ranks], refs[ranks:]
        slope_refs, refs = refs[:ranks], refs[ranks:]
        dots_refs, refs = refs[:ranks], refs[ranks:]
        flat, (out_ref, first, second, sem) = refs[: sum(counts)], refs[sum(counts) :]
        sources = [flat[: counts[0]], flat[counts[0] :]]
        held = [first, second]
        fills = [[] for _ in range(steps)]
        number = 0
        for step in range(steps):
            for who in range(ranks):
                for which, start, to, many in layouts[who]:
                    if to // depth == step:
                        fills[step].append(
                            pltpu.make_async_copy(
                                sources[who][which].at[pl.ds(start, many), :],
                                held[who].at[pl.ds(to, many), :],
                                sem.at[number],
                            )
                        )
                        number += 1
        for group in fills:
            for copy in group:
                copy.start()
        picks = []
        for b in range(blocks):
            hits = []
            for who in range(ranks):
                for n in range(local):
                    row = (part * blocks + b) * local + n
                    hits.append(chosen(at_refs[who][row : row + 1, :], ROOM).astype(F32))
            picks.append(jnp.concatenate(hits, axis=0).astype(BF16))
        lines = lax.broadcasted_iota(jnp.int32, (EXTRA, size), 0)
        for b in range(blocks):
            values = []
            for who in range(ranks):
                for n in range(local):
                    row = (part * blocks + b) * local + n
                    value = dots_refs[who][row : row + 1, :]
                    high = value.astype(BF16).astype(F32)
                    values.append((owner_ref[who * local + n], high, value - high))
            for lane in range(N_DP):
                tile = jnp.zeros((EXTRA, size), F32)
                for slot, high, low in values:
                    line = jnp.where(slot % N_DP == lane, slot // N_DP, EXTRA)
                    tile = jnp.where(lines == line, high, tile)
                    tile = jnp.where(lines == line + 2, low, tile)
                place = slice(b * tall + 2 * size, (b + 1) * tall)
                out_ref[place, lane * size : (lane + 1) * size] = tile.astype(BF16)
        for step in range(steps):
            for copy in fills[step]:
                copy.wait()
            span = slice(step * depth, (step + 1) * depth)
            for side in (0, 1):
                made = []
                for who in range(ranks):
                    for n in range(local):
                        begin = n * every + part * rows
                        left = (hid_refs, slope_refs)[side][who][begin : begin + rows, :]
                        column = ((1 - side) * local + n) * hidden
                        made.append(dot(left, held[who][span, column : column + hidden], COLS).astype(BF16))
                for b in range(blocks):
                    stack = jnp.concatenate([m[b * ROOM : (b + 1) * ROOM] for m in made], axis=0)
                    begin = b * tall + side * size
                    out_ref[begin : begin + size, span] = dot(picks[b], stack, ROWS).astype(BF16)

    entries = sum(len(layout) for layout in layouts)
    return call(
        body,
        [SCALARS] + [NEAR] * (4 * ranks) + [AWAY] * sum(counts),
        [(NEAR, jax.ShapeDtypeStruct((blocks * tall, width), BF16))],
        4 * ranks * local * rows * width * (hidden + size) * SCALE,
        4 * blocks * size * width + 4 * width * cut * ranks,
        [pltpu.VMEM((width, 2 * cut), BF16)] * 2 + [pltpu.SemaphoreType.DMA((entries,))],
    )(owners, *ats, *hids, *slopes, *dots, *[w for some in weights for w in some])[0]


def weight_grads(toks, grds, hid, slope, local, order):
    tall, width = toks.shape
    hidden = hid.shape[1]
    rows = tall // local
    size = width // N_DP
    group = 4
    steps = len(order) // group

    def body(*refs):
        ins, (hid_ref, slope_ref, out_ref) = refs[:-3], refs[-3:]
        for side, other in ((0, slope_ref), (1, hid_ref)):
            these = ins[side * group : (side + 1) * group]
            for n in range(local):
                mine = slice(n * rows, (n + 1) * rows)
                left = jnp.concatenate([r[mine, :] for r in these], axis=1)
                span = slice((side * local + n) * hidden, (side * local + n + 1) * hidden)
                out_ref[:, span] = dot(left, other[mine, :], ROWS).astype(BF16)

    def spec(n):
        places = [order[step * group + n] for step in range(steps)]

        def index(i):
            here = places[0]
            for step in range(1, steps):
                here = jnp.where(i == step, places[step], here)
            return (0, here)

        return pl.BlockSpec((tall, size), index)

    whole = pl.BlockSpec(hid.shape, lambda i: (0, 0), pipeline_mode=pl.Buffered(1))
    out = pl.BlockSpec((group * size, 2 * local * hidden), lambda i: (i, 0))
    return call(
        body,
        [spec(n) for n in range(group)] * 2 + [whole, whole],
        [(out, jax.ShapeDtypeStruct((len(order) * size, 2 * local * hidden), BF16))],
        4 * tall * len(order) * size * hidden * SCALE,
        4 * tall * (len(order) * size + hidden) + 4 * len(order) * size * local * hidden,
        (),
        (steps,),
    )(*[toks] * group, *[grds] * group, hid, slope)[0]


def per_device(tokens, grad_out, routes, probs, old_place, new_place, gate_w, gate_m, gate_v, down_w, down_m, down_v):
    tok_rows, width = tokens.shape
    experts = old_place.shape[0]
    local_count, shard, hidden = gate_w.shape
    ep, dp = lax.axis_index("ep"), lax.axis_index("dp")
    y, zl = ep // N_ZL, ep % N_ZL
    zb, za = zl // 2, zl % 2
    zh, c = dp // N_C % N_ZH, dp % N_C
    slots = jnp.arange(experts, dtype=jnp.int32)
    place = jnp.stack([zh, c]).astype(jnp.int32)

    inverse = jnp.sum(jnp.where(old_place[None, :] == slots[:, None], slots[None, :], 0), axis=1)
    slot = jnp.sum(jnp.where(routes[:, :, None] == slots, inverse, 0), axis=2)
    hits = slot.T[None] == slots[:, None, None]
    by_slot = jnp.sum(jnp.where(hits, probs.T[None], 0.0), axis=1)
    named = jnp.any(hits, axis=1)
    before = jnp.arange(tok_rows)[:, None] < jnp.arange(tok_rows)[None, :]
    number = jnp.where(named, dot(named.astype(BF16), before.astype(BF16)), -1.0)
    high = by_slot.astype(BF16)
    low = (by_slot - high.astype(F32)).astype(BF16)
    table = jnp.concatenate([number.astype(BF16), high, low], axis=0).reshape(-1, width)
    table = jnp.pad(table, ((0, EXTRA - table.shape[0]), (0, 0)))
    here = pack(place, tokens, grad_out, table)

    def side(state):
        return jnp.transpose(state, (0, 2, 1))

    weights = [gate_w, side(down_w)]
    block = jnp.concatenate([state[n] for state in weights for n in range(local_count)], axis=1)

    def gather_x(rows):
        return lax.all_gather(rows, "dp", axis=0, tiled=True, axis_index_groups=X_GROUPS)

    own_rows = gather_x(block)
    z_left, z_right = send(block, Z_UP), send(block, Z_DOWN)
    up, down, pair = send(here, Y_UP), send(here, Y_DOWN), send(here, Z_PAIR)
    z_left, z_right, up, down, pair, here, block, own_rows = lax.optimization_barrier(
        (z_left, z_right, up, down, pair, here, block, own_rows)
    )
    near = jnp.concatenate([jnp.where(zb == 1, z_left, z_right), jnp.where(zb == 1, z_right, z_left)], axis=0)
    near_rows = gather_x(near)
    far = send(block, Z_FAR)
    pair_up, pair_down = send(pair, Y_UP), send(pair, Y_DOWN)
    far_tok, far_grd = send(up[:tok_rows], Y_UP), send(down[tok_rows:], Y_DOWN)
    far, pair_up, pair_down, far_tok, far_grd, near_rows = lax.optimization_barrier(
        (far, pair_up, pair_down, far_tok, far_grd, near_rows)
    )
    pair_far_tok, pair_far_grd = send(pair_up[:tok_rows], Y_UP), send(pair_down[tok_rows:], Y_DOWN)
    far_rows = gather_x(far)
    near_weights = [near_rows, send(near_rows, CORE)]
    own_weights = [own_rows, send(own_rows, CORE)]
    blocks = []
    for three, tok, grd in (
        ((here, up, down), far_tok, far_grd),
        ((pair, pair_up, pair_down), pair_far_tok, pair_far_grd),
    ):
        blocks += [((a, 0), (a, tok_rows)) for a in three] + [((tok, 0), (grd, 0))]
    owners = [
        jnp.stack([((y * 2 + (zb ^ who)) * 2 + za) * local_count + n for n in range(local_count)]) for who in (0, 1)
    ]

    span = N_X * shard
    own_layout = [(j * N_C + k, 0, (j * N_C + k) * span, span) for j in range(N_ZH) for k in range(N_C)]
    near_layout = [
        (k, (i * N_ZH + j) * shard, (j * N_C + k) * span + i * shard, shard)
        for j in range(N_ZH)
        for k in range(N_C)
        for i in range(N_X)
    ]

    near_x, near_g, near_hid, near_slope, near_dots, near_at = inner(
        blocks, owners[1], near_weights, near_layout, hidden
    )

    def scatter_core(x, g, hid, slope, order):
        theirs = weight_grads(x, g, hid, slope, local_count, [n(1) for n in order])
        theirs = send(theirs, CORE)
        return weight_grads(x, g, hid, slope, local_count, [n(0) for n in order]), theirs

    def scatter_x(both):
        return lax.psum_scatter(both, "dp", scatter_dimension=0, tiled=True, axis_index_groups=X_GROUPS)

    def at(j, i):
        return lambda k: (j * N_C + k) * N_X + i

    ours, theirs = scatter_core(
        near_x, near_g, near_hid, near_slope, [at(j, i) for i in range(N_X) for j in range(N_ZH)]
    )
    near_sum = add(ours, theirs)

    changed = new_place != old_place
    source = jnp.sum(jnp.where(new_place[:, None] == old_place[None, :], slots[None, :], 0), axis=1)
    first = changed & (source // local_count == (slots // local_count - 1) % N_EP)
    root = jnp.sum(jnp.where(first, slots // local_count, 0))
    mine = [jnp.any(changed & (slots == ep * local_count + n)) for n in range(local_count)]

    def migrate(payload):
        def branch(rank):
            stops = [(rank - 1) % N_EP, rank, (rank - 1 - N_EP // 2) % N_EP, (rank - 1) % N_EP]
            pairs = [(stops[0], stops[1]), (stops[2], stops[3]), (stops[1], stops[2])]
            return lambda part: lax.ppermute(part, "ep", pairs)

        return lax.switch(root, [branch(rank) for rank in range(N_EP)], payload)

    def leaving(states):
        return jnp.concatenate([jnp.where(mine[1], state[1], state[0]) for state in states], axis=1)

    states = [gate_w, gate_m, gate_v, down_w, down_m, down_v]
    payload = after(leaving([gate_w, gate_m, gate_v] + [side(state) for state in states[3:]]), near_hid)
    arrivals = [send_ep(payload, pairs) for pairs in (E_NEXT, E_HALF, E_BACK)]
    far_rows, owners[0], near_sum, *arrivals = lax.optimization_barrier((far_rows, owners[0], near_sum, *arrivals))
    own_weights += [far_rows, send(far_rows, CORE)]
    near_grads = scatter_x(near_sum)
    own_x, own_g, own_hid, own_slope, own_dots, own_at = inner(
        blocks, owners[0], own_weights, own_layout, hidden
    )
    ours, theirs = scatter_core(
        own_x, own_g, own_hid, own_slope, [at(j, i) for i in range(N_X) for j in range(N_ZH)]
    )
    own_sum = add(ours, theirs)
    own_grads = scatter_x(own_sum)

    owners = jnp.concatenate(owners)

    def made(part, *others):
        return outer(
            after(owners, *others),
            [own_at, near_at],
            [own_hid, near_hid],
            [own_slope, near_slope],
            [own_dots, near_dots],
            [own_weights, near_weights],
            [own_layout, near_layout],
            part,
            2,
        )

    def cut_up(rows):
        tall = 2 * tok_rows + EXTRA
        return [rows[n * tall : (n + 1) * tall] for n in range(4)]

    def halves(far):
        return send(far[:tok_rows], Y_UP), send(far[tok_rows:], Y_DOWN)

    def passed(left, right, from_left, from_right):
        right = jnp.concatenate([add(right[:tok_rows], from_left), right[tok_rows:]], axis=0)
        left = jnp.concatenate([left[:tok_rows], add(left[tok_rows:], from_right)], axis=0)
        return left, right

    rows = made(1, own_sum)
    rows, near_grads = lax.optimization_barrier((rows, near_grads))
    mine_late, left, right, far = cut_up(rows)
    far_late = halves(far)
    next_rows = made(0, rows)
    far_late, left, right, next_rows, near_grads, place = lax.optimization_barrier(
        (far_late, left, right, next_rows, near_grads, place)
    )
    mine_soon, next_left, next_right, next_far = cut_up(next_rows)
    near_grads = [near_grads[:shard], near_grads[shard:]]
    to_right = jnp.where(zb == 1, near_grads[1], near_grads[0])
    to_left = jnp.where(zb == 1, near_grads[0], near_grads[1])
    from_z = [send(to_right, Z_UP), send(to_left, Z_DOWN)]
    left, right = passed(left, right, *far_late)
    late = [mine_late, send(right, Y_UP), send(left, Y_DOWN)]
    next_far, next_left, next_right, late, from_z, own_grads, place = lax.optimization_barrier(
        (next_far, next_left, next_right, late, from_z, own_grads, hold(place))
    )
    from_z.append(send(own_grads[shard:], Z_FAR))
    other = functools.reduce(lambda a, b: a + b, [p.astype(F32) for p in late]).astype(BF16)
    from_pair = send(other, Z_PAIR)
    left, right = passed(next_left, next_right, *halves(next_far))
    mixed, grad_tokens, table = total(place, mine_soon, send(right, Y_UP), send(left, Y_DOWN), from_pair)
    table = table[: 2 * experts // N_DP].reshape(2, experts, tok_rows)
    grad_probs = jnp.sum(jnp.where(hits, (table[0] + table[1])[:, None, :], 0.0), axis=0).T

    terms = [own_grads[:shard], *from_z]
    grad = functools.reduce(lambda a, b: a + b, [term.astype(F32) for term in terms])

    grads = [[grad[:, (s * local_count + n) * hidden :][:, :hidden] for n in range(local_count)] for s in (0, 1)]
    moved = migrate(leaving(grads).astype(BF16))
    arrived = jnp.where(ep == root, arrivals[0], jnp.where(ep == (root - 1) % N_EP, arrivals[1], arrivals[2]))
    mine = jnp.stack(mine).astype(jnp.int32)
    return (mixed, grad_tokens, grad_probs, *updates(mine, grad, moved, states, arrived))


def solution(mesh):
    tok = P(("ep", "dp"), None)
    gate, down = P("ep", "dp", None), P("ep", None, "dp")
    in_specs = (tok, tok, tok, tok, P(), P(), gate, gate, gate, down, down, down)
    out_specs = (tok, tok, tok, gate, gate, gate, down, down, down)
    return jax.shard_map(per_device, mesh=mesh, in_specs=in_specs, out_specs=out_specs, check_vma=False)
```

```python
import functools
import jax
import jax.numpy as jnp
from jax import lax
from jax.experimental import pallas as pl
from jax.experimental.pallas import tpu as pltpu
from jax.sharding import PartitionSpec as P

beta_one = 0.9
beta_two = 0.95
step_rate = 0.001
adam_eps = 1e-08

BOTH = ("ep", "dp")
N_Y, N_ZL, N_X, N_ZH, N_C = 4, 4, 4, 2, 2
N_EP, N_DP = N_Y * N_ZL, N_X * N_ZH * N_C
F32, BF16 = jnp.float32, jnp.bfloat16


def links(move):
    pairs = []
    for ep in range(N_EP):
        for dp in range(N_DP):
            y, zl = divmod(ep, N_ZL)
            x, rest = divmod(dp, N_ZH * N_C)
            zh, c = divmod(rest, N_C)
            y, x, z, c = move(y, x, zh * N_ZL + zl, c)
            zh, zl = divmod(z % (N_ZH * N_ZL), N_ZL)
            there = (y % N_Y * N_ZL + zl) * N_DP + x % N_X * N_ZH * N_C + zh * N_C + c
            pairs.append((ep * N_DP + dp, there))
    return pairs


Y_UP = links(lambda y, x, z, c: (y + 1, x, z, c))
Y_DOWN = links(lambda y, x, z, c: (y - 1, x, z, c))
X_UP = links(lambda y, x, z, c: (y, x + 1, z, c))
X_DOWN = links(lambda y, x, z, c: (y, x - 1, z, c))
Z_UP = links(lambda y, x, z, c: (y, x, z + 2, c))
Z_DOWN = links(lambda y, x, z, c: (y, x, z - 2, c))
Z_PAIR = links(lambda y, x, z, c: (y, x, z ^ 1, c))
Z_FAR = links(lambda y, x, z, c: (y, x, z + 4, c))
X_GROUPS = [[i * N_ZH * N_C + rest for i in range(N_X)] for rest in range(N_ZH * N_C)]
ROOM = 48
EXTRA = 16
VMEM = 56 * 2**20
SHORT, LONG = 10**9, 10**12
CORE = links(lambda y, x, z, c: (y, x, z, 1 - c))


E_NEXT = [(rank, (rank + 1) % N_EP) for rank in range(N_EP)]
E_HALF = [(rank, (rank + N_EP // 2) % N_EP) for rank in range(N_EP)]
E_PREV = [(rank, (rank - 1) % N_EP) for rank in range(N_EP)]


def after(array, *others):
    return lax.optimization_barrier((array, *others))[0]


def send(block, pairs):
    return lax.ppermute(block, BOTH, pairs)


def send_ep(block, pairs):
    return lax.ppermute(block, "ep", pairs)


def add(first, second):
    return (first.astype(F32) + second.astype(F32)).astype(BF16)


def adam_update(weight, first, second, grad):
    first_new = beta_one * first.astype(F32) + (1.0 - beta_one) * grad
    second_new = beta_two * second.astype(F32) + (1.0 - beta_two) * grad * grad
    weight_new = weight.astype(F32) - step_rate * first_new / (jnp.sqrt(second_new) + adam_eps)
    return weight_new.astype(BF16), first_new.astype(BF16), second_new.astype(BF16)


def updates(mine, grad, moved, states, arrived):
    local, shard, hidden = states[0].shape

    def body(mine_ref, grad_ref, moved_ref, *refs):
        ins, arrived_ref, outs = refs[:6], refs[6], refs[7:]
        for n in range(local):
            here = mine_ref[n] > 0
            for side in (0, 1):
                span = slice((side * local + n) * hidden, (side * local + n + 1) * hidden)
                value = jnp.where(here, moved_ref[:, side * hidden : (side + 1) * hidden].astype(F32), grad_ref[:, span])
                if side:
                    value = value.T
                state = []
                for kind in range(3):
                    column = (side * 3 + kind) * hidden
                    fresh = arrived_ref[:, column : column + hidden].astype(F32)
                    old = ins[side * 3 + kind][n].astype(F32)
                    state.append(jnp.where(here, fresh.T if side else fresh, old))
                for kind, done in enumerate(adam_update(*state, value)):
                    outs[side * 3 + kind][n] = done

    shapes = [jax.ShapeDtypeStruct(state.shape, BF16) for state in states]
    moved_bytes = 4 * 6 * local * shard * hidden
    return call(
        body, [SCALARS] + [NEAR] * 9, [(NEAR, shape) for shape in shapes], 0, moved_bytes
    )(mine, grad, moved, *states, arrived)


def dot(left, right, dims=((1,), (0,))):
    return lax.dot_general(left, right, (dims, ((), ())), preferred_element_type=F32)


COLS = ((1,), (1,))
ROWS = ((0,), (0,))
NEAR = pl.BlockSpec(memory_space=pltpu.VMEM)
AWAY = pl.BlockSpec(memory_space=pl.ANY)
SCALARS = pl.BlockSpec(memory_space=pltpu.SMEM)


def call(body, ins, outs, flops, moved, scratch=(), grid=()):
    return pl.pallas_call(
        body,
        grid=grid,
        in_specs=list(ins),
        out_specs=[spec for spec, _ in outs],
        out_shape=[shape for _, shape in outs],
        scratch_shapes=list(scratch),
        compiler_params=pltpu.CompilerParams(vmem_limit_bytes=VMEM),
        cost_estimate=pl.CostEstimate(flops=flops, bytes_accessed=moved, transcendentals=0),
    )


def relative(n, zh, c):
    j, k, i = n // (N_C * N_X), n // N_X % N_C, n % N_X
    return (i * N_ZH + (j ^ zh)) * N_C + (k ^ c)


def pack(place, tokens, grads, table):
    rows, width = tokens.shape
    block = width // N_DP

    def body(place_ref, tok_ref, grd_ref, table_ref, out_ref):
        zh, c = place_ref[0], place_ref[1]
        for n in range(N_DP):
            at = pl.multiple_of(relative(n, zh, c) * block, block)
            here = slice(n * block, (n + 1) * block)
            out_ref[:rows, here] = tok_ref[:, pl.ds(at, block)]
            out_ref[rows : 2 * rows, here] = grd_ref[:, pl.ds(at, block)]
        out_ref[2 * rows :, :] = table_ref[...]

    shape = jax.ShapeDtypeStruct((2 * rows + EXTRA, width), BF16)
    return call(body, [SCALARS] + [NEAR] * 3, [(NEAR, shape)], 0, 8 * rows * width)(place, tokens, grads, table)[0]


def total(place, *arrays):
    rows, width = arrays[0].shape
    rows = (rows - EXTRA) // 2
    block = width // N_DP

    def body(place_ref, *refs):
        zh, c = place_ref[0], place_ref[1]
        ins, (mixed_ref, back_ref, table_ref) = refs[:-3], refs[-3:]

        def added(at, here):
            value = ins[0][at, here].astype(F32)
            for source in ins[1:]:
                value = value + source[at, here].astype(F32)
            return value

        for n in range(N_DP):
            at = pl.multiple_of(relative(n, zh, c) * block, block)
            here = slice(n * block, (n + 1) * block)
            mixed_ref[:, pl.ds(at, block)] = added(slice(0, rows), here).astype(BF16)
            back_ref[:, pl.ds(at, block)] = added(slice(rows, 2 * rows), here).astype(BF16)
        table_ref[...] = added(slice(2 * rows, 2 * rows + EXTRA), slice(0, width))

    outs = [(NEAR, jax.ShapeDtypeStruct((rows, width), BF16))] * 2
    outs.append((NEAR, jax.ShapeDtypeStruct((EXTRA, width), F32)))
    return call(body, [SCALARS] + [NEAR] * len(arrays), outs, 0, 20 * rows * width)(place, *arrays)


def hold(place):
    def body(place_ref, out_ref):
        for n in range(2):
            out_ref[n] = place_ref[n]

    return call(body, [SCALARS], [(SCALARS, jax.ShapeDtypeStruct(place.shape, place.dtype))], 2**40, 0)(place)[0]


def passed(left, right, from_left, from_right):
    size = from_left.shape[0]
    width = left.shape[1]

    def body(left_ref, right_ref, from_left_ref, from_right_ref, left_out, right_out):
        left_out[:size] = left_ref[:size]
        left_out[size:] = add(left_ref[size:], from_right_ref[...])
        right_out[:size] = add(right_ref[:size], from_left_ref[...])
        right_out[size:] = right_ref[size:]

    tile = width // 4
    down = lambda array: pl.BlockSpec((array.shape[0], tile), lambda i: (0, i))
    arrays = (left, right, from_left, from_right)
    shape = jax.ShapeDtypeStruct(left.shape, BF16)
    return call(body, [down(a) for a in arrays], [(down(left), shape)] * 2, 0, 0, (), (4,))(*arrays)


def chosen(at, rows):
    return lax.broadcasted_iota(jnp.int32, (rows, at.shape[1]), 0).astype(F32) == at


def inner(blocks, owners, weights, layout, hidden, cost):
    count = len(blocks)
    size, width = blocks[0][0][0].shape[1] // N_DP, blocks[0][0][0].shape[1]
    local = owners.shape[0]
    cut = local * hidden
    rows = count * ROOM
    arrays = []
    for block in blocks:
        for array, _ in block:
            if not any(array is other for other in arrays):
                arrays.append(array)
    index = lambda array: next(n for n, other in enumerate(arrays) if other is array)
    starts = [[(index(array), start) for array, start in block] for block in blocks]
    spans = [(side * local + n) * hidden for n in range(local) for side in (0, 1)]

    def body(owner_ref, *refs):
        sources, stored = refs[: len(arrays)], refs[len(arrays) : len(arrays) + len(weights)]
        x_ref, g_ref, hid_ref, slope_ref, dots_ref, at_ref, held, tables, weight, sem, weight_sem = refs[
            len(arrays) + len(weights) :
        ]
        moves, fills = [], []
        for b, block in enumerate(starts):
            moves.append(
                [
                    pltpu.make_async_copy(
                        sources[which].at[pl.ds(start, size), :],
                        held.at[b, pl.ds(side * size, size), :],
                        sem.at[2 * b + side],
                    )
                    for side, (which, start) in enumerate(block)
                ]
            )
            which, start = block[1]
            moves[b].append(
                pltpu.make_async_copy(
                    sources[which].at[pl.ds(start + size, EXTRA), :], tables.at[b], sem.at[2 * count + b]
                )
            )
        for number, span in enumerate(spans):
            fills.append(
                [
                    pltpu.make_async_copy(
                        stored[which].at[pl.ds(start, depth), pl.ds(span, hidden)],
                        weight.at[pl.ds(to, depth), pl.ds(span, hidden)],
                        weight_sem.at[number * len(layout) + entry],
                    )
                    for entry, (which, start, to, depth) in enumerate(layout)
                ]
            )
        for group in moves + fills:
            for copy in group:
                copy.start()
        factors = [[] for _ in range(local)]
        lines = lax.broadcasted_iota(jnp.int32, (EXTRA, size), 0)
        for b in range(count):
            for copy in moves[b]:
                copy.wait()
            hits = []
            for n in range(local):
                slot = owner_ref[n]
                lanes = pl.ds(pl.multiple_of(slot % N_DP * size, size), size)
                tile = tables[b, :, lanes].astype(F32)
                line = slot // N_DP
                entry = lambda kind: jnp.sum(jnp.where(lines == line + 2 * kind, tile, 0.0), axis=0, keepdims=True)
                number = entry(0)
                at_ref[b * local + n : b * local + n + 1, :] = number
                hits.append(chosen(number, ROOM))
                factors[n].append(jnp.sum(jnp.where(hits[n], entry(1) + entry(2), 0.0), axis=1, keepdims=True))
            pick = jnp.concatenate([hit.astype(F32) for hit in hits], axis=0).astype(BF16)
            for side, target in enumerate((x_ref, g_ref)):
                got = dot(pick, held[b, side * size : (side + 1) * size, :]).astype(BF16)
                for n in range(local):
                    target[n * rows + b * ROOM : n * rows + (b + 1) * ROOM, :] = got[n * ROOM : (n + 1) * ROOM]
        for n in range(local):
            for copy in fills[2 * n] + fills[2 * n + 1]:
                copy.wait()
            mine = slice(n * rows, (n + 1) * rows)
            here = dot(x_ref[mine, :], weight[:, n * hidden : (n + 1) * hidden])
            over = dot(g_ref[mine, :], weight[:, cut + n * hidden : cut + (n + 1) * hidden])
            factor = jnp.concatenate(factors[n], axis=0)
            sigmoid = jax.nn.sigmoid(here)
            act = here * sigmoid
            hid_ref[mine, :] = (factor * act).astype(BF16)
            slope_ref[mine, :] = (factor * over * (sigmoid + act * (1.0 - sigmoid))).astype(BF16)
            sums = jnp.sum(act * over, axis=1, keepdims=True)
            for b in range(count):
                hit = chosen(at_ref[b * local + n : b * local + n + 1, :], ROOM)
                spread = jnp.where(hit, sums[b * ROOM : (b + 1) * ROOM], 0.0)
                dots_ref[b * local + n : b * local + n + 1, :] = jnp.sum(spread, axis=0, keepdims=True)

    shape = lambda last, kind: jax.ShapeDtypeStruct((local * rows, last), kind)
    outs = [(NEAR, shape(width, BF16))] * 2 + [(NEAR, shape(hidden, BF16))] * 2
    outs += [(NEAR, jax.ShapeDtypeStruct((count * local, size), F32))] * 2
    return call(
        body,
        [SCALARS] + [AWAY] * (len(arrays) + len(weights)),
        outs,
        cost,
        1,
        [
            pltpu.VMEM((count, 2 * size, width), BF16),
            pltpu.VMEM((count, EXTRA, width), BF16),
            pltpu.VMEM((width, 2 * cut), BF16),
            pltpu.SemaphoreType.DMA((3 * count,)),
            pltpu.SemaphoreType.DMA((len(spans) * len(layout),)),
        ],
    )(owners, *arrays, *weights)


def outer(owners, ats, hids, slopes, dots, weights, layouts, part, parts, cost):
    ranks = len(hids)
    size = ats[0].shape[1]
    local = owners.shape[0] // ranks
    hidden = hids[0].shape[1]
    cut = local * hidden
    every = hids[0].shape[0] // local
    rows = every // parts
    blocks = rows // ROOM
    width = size * N_DP
    steps = N_ZH * N_C
    depth = width // steps
    counts = [len(some) for some in weights]
    tall = 2 * size + EXTRA

    def target(outs, b, piece):
        if b < blocks - 1:
            return outs[b], piece * size
        return (outs[b], 0) if piece == 0 else (outs[b + 1], (piece - 1) * size)

    def body(owner_ref, *refs):
        at_refs, refs = refs[:ranks], refs[ranks:]
        hid_refs, refs = refs[:ranks], refs[ranks:]
        slope_refs, refs = refs[:ranks], refs[ranks:]
        dots_refs, refs = refs[:ranks], refs[ranks:]
        flat, outs, (first, second, sem) = refs[: sum(counts)], refs[sum(counts) : -3], refs[-3:]
        sources = [flat[: counts[0]], flat[counts[0] :]]
        held = [first, second]
        fills = [[] for _ in range(steps)]
        number = 0
        for step in range(steps):
            for who in range(ranks):
                for which, start, to, many in layouts[who]:
                    if to // depth == step:
                        fills[step].append(
                            pltpu.make_async_copy(
                                sources[who][which].at[pl.ds(start, many), :],
                                held[who].at[pl.ds(to, many), :],
                                sem.at[number],
                            )
                        )
                        number += 1
        for group in fills:
            for copy in group:
                copy.start()
        picks = []
        for b in range(blocks):
            hits = []
            for who in range(ranks):
                for n in range(local):
                    row = (part * blocks + b) * local + n
                    hits.append(chosen(at_refs[who][row : row + 1, :], ROOM).astype(F32))
            picks.append(jnp.concatenate(hits, axis=0).astype(BF16))
        lines = lax.broadcasted_iota(jnp.int32, (EXTRA, size), 0)
        for b in range(blocks):
            values = []
            for who in range(ranks):
                for n in range(local):
                    row = (part * blocks + b) * local + n
                    value = dots_refs[who][row : row + 1, :]
                    high = value.astype(BF16).astype(F32)
                    values.append((owner_ref[who * local + n], high, value - high))
            for lane in range(N_DP):
                tile = jnp.zeros((EXTRA, size), F32)
                for slot, high, low in values:
                    line = jnp.where(slot % N_DP == lane, slot // N_DP, EXTRA)
                    tile = jnp.where(lines == line, high, tile)
                    tile = jnp.where(lines == line + 2, low, tile)
                out_ref, begin = target(outs, b, 2)
                out_ref[begin : begin + EXTRA, lane * size : (lane + 1) * size] = tile.astype(BF16)
        for step in range(steps):
            for copy in fills[step]:
                copy.wait()
            span = slice(step * depth, (step + 1) * depth)
            for side in (0, 1):
                made = []
                for who in range(ranks):
                    for n in range(local):
                        begin = n * every + part * rows
                        left = (hid_refs, slope_refs)[side][who][begin : begin + rows, :]
                        column = ((1 - side) * local + n) * hidden
                        made.append(dot(left, held[who][span, column : column + hidden], COLS).astype(BF16))
                for b in range(blocks):
                    stack = jnp.concatenate([m[b * ROOM : (b + 1) * ROOM] for m in made], axis=0)
                    out_ref, begin = target(outs, b, side)
                    out_ref[begin : begin + size, span] = dot(picks[b], stack, ROWS).astype(BF16)

    entries = sum(len(layout) for layout in layouts)
    return call(
        body,
        [SCALARS] + [NEAR] * (4 * ranks) + [AWAY] * sum(counts),
        [
            (NEAR, jax.ShapeDtypeStruct((many, width), BF16))
            for many in [tall] * (blocks - 1) + [size, tall - size]
        ],
        cost,
        1,
        [pltpu.VMEM((width, 2 * cut), BF16)] * 2 + [pltpu.SemaphoreType.DMA((entries,))],
    )(owners, *ats, *hids, *slopes, *dots, *[w for some in weights for w in some])


def weight_grads(toks, grds, hid, slope, local, order, cost, theirs=None):
    tall, width = toks.shape
    hidden = hid.shape[1]
    rows = tall // local
    size = width // N_DP
    group = 4
    steps = len(order) // group

    def body(*refs):
        ins, (hid_ref, slope_ref, *theirs_ref, out_ref) = refs[: 2 * group], refs[2 * group :]
        for side, other in ((0, slope_ref), (1, hid_ref)):
            these = ins[side * group : (side + 1) * group]
            for n in range(local):
                mine = slice(n * rows, (n + 1) * rows)
                left = jnp.concatenate([r[mine, :] for r in these], axis=1)
                span = slice((side * local + n) * hidden, (side * local + n + 1) * hidden)
                value = dot(left, other[mine, :], ROWS)
                for more in theirs_ref:
                    value = value + more[:, span].astype(F32)
                out_ref[:, span] = value.astype(BF16)

    def spec(n):
        places = [order[step * group + n] for step in range(steps)]

        def index(i):
            here = places[0]
            for step in range(1, steps):
                here = jnp.where(i == step, places[step], here)
            return (0, here)

        return pl.BlockSpec((tall, size), index)

    whole = pl.BlockSpec(hid.shape, lambda i: (0, 0), pipeline_mode=pl.Buffered(1))
    out = pl.BlockSpec((group * size, 2 * local * hidden), lambda i: (i, 0))
    extra = [] if theirs is None else [theirs]
    return call(
        body,
        [spec(n) for n in range(group)] * 2 + [whole, whole] + [out] * len(extra),
        [(out, jax.ShapeDtypeStruct((len(order) * size, 2 * local * hidden), BF16))],
        cost,
        1,
        (),
        (steps,),
    )(*[toks] * group, *[grds] * group, hid, slope, *extra)[0]


def per_device(tokens, grad_out, routes, probs, old_place, new_place, gate_w, gate_m, gate_v, down_w, down_m, down_v):
    tok_rows, width = tokens.shape
    experts = old_place.shape[0]
    local_count, shard, hidden = gate_w.shape
    ep, dp = lax.axis_index("ep"), lax.axis_index("dp")
    y, zl = ep // N_ZL, ep % N_ZL
    zb, za = zl // 2, zl % 2
    zh, c = dp // N_C % N_ZH, dp % N_C
    slots = jnp.arange(experts, dtype=jnp.int32)
    place = jnp.stack([zh, c]).astype(jnp.int32)

    inverse = jnp.sum(jnp.where(old_place[None, :] == slots[:, None], slots[None, :], 0), axis=1)
    slot = jnp.sum(jnp.where(routes[:, :, None] == slots, inverse, 0), axis=2)
    hits = slot.T[None] == slots[:, None, None]
    by_slot = jnp.sum(jnp.where(hits, probs.T[None], 0.0), axis=1)
    named = jnp.any(hits, axis=1)
    before = jnp.arange(tok_rows)[:, None] < jnp.arange(tok_rows)[None, :]
    number = jnp.where(named, dot(named.astype(BF16), before.astype(BF16)), -1.0)
    high = by_slot.astype(BF16)
    low = (by_slot - high.astype(F32)).astype(BF16)
    table = jnp.concatenate([number.astype(BF16), high, low], axis=0).reshape(-1, width)
    table = jnp.pad(table, ((0, EXTRA - table.shape[0]), (0, 0)))
    here = pack(place, tokens, grad_out, table)

    def side(state):
        return jnp.transpose(state, (0, 2, 1))

    weights = [gate_w, side(down_w)]
    block = jnp.concatenate([state[n] for state in weights for n in range(local_count)], axis=1)

    def gather_x(rows):
        return lax.all_gather(rows, "dp", axis=0, tiled=True, axis_index_groups=X_GROUPS)

    changed = new_place != old_place
    source = jnp.sum(jnp.where(new_place[:, None] == old_place[None, :], slots[None, :], 0), axis=1)
    first = changed & (source // local_count == (slots // local_count - 1) % N_EP)
    root = jnp.sum(jnp.where(first, slots // local_count, 0))
    mine = [jnp.any(changed & (slots == ep * local_count + n)) for n in range(local_count)]

    def migrate(payload):
        def branch(rank):
            stops = [(rank - 1) % N_EP, rank, (rank - 1 - N_EP // 2) % N_EP, (rank - 1) % N_EP]
            pairs = [(stops[0], stops[1]), (stops[2], stops[3]), (stops[1], stops[2])]
            return lambda part: lax.ppermute(part, "ep", pairs)

        return lax.switch(root, [branch(rank) for rank in range(N_EP)], payload)

    def leaving(states):
        return jnp.concatenate([jnp.where(mine[1], state[1], state[0]) for state in states], axis=1)

    states = [gate_w, gate_m, gate_v, down_w, down_m, down_v]
    payload = leaving([gate_w, gate_m, gate_v] + [side(state) for state in states[3:]])

    own_rows = gather_x(block)
    block = after(block, here)
    z_left, z_right = send(block, Z_UP), send(block, Z_DOWN)
    up, down = send(here, Y_UP), send(here, Y_DOWN)
    z_left, z_right, up, down, here, block, own_rows, payload = lax.optimization_barrier(
        (z_left, z_right, up, down, here, block, own_rows, payload)
    )
    near = jnp.concatenate([jnp.where(zb == 1, z_left, z_right), jnp.where(zb == 1, z_right, z_left)], axis=0)
    near_rows = gather_x(near)
    pair = send(here, Z_PAIR)
    far_tok, far_grd = send(up[:tok_rows], Y_UP), send(down[tok_rows:], Y_DOWN)
    across = send_ep(payload, E_HALF)
    pair, far_tok, far_grd, block, across = lax.optimization_barrier((pair, far_tok, far_grd, block, across))
    pair_up, pair_down = send(pair, Y_UP), send(pair, Y_DOWN)
    far = send(block, Z_FAR)
    pair_up, pair_down, far, near_rows = lax.optimization_barrier((pair_up, pair_down, far, near_rows))
    pair_far_tok, pair_far_grd = send(pair_up[:tok_rows], Y_UP), send(pair_down[tok_rows:], Y_DOWN)
    far_rows = gather_x(far)
    near_weights = [near_rows, send(near_rows, CORE)]
    own_weights = [own_rows, send(own_rows, CORE)]
    blocks = []
    for three, tok, grd in (
        ((here, up, down), far_tok, far_grd),
        ((pair, pair_up, pair_down), pair_far_tok, pair_far_grd),
    ):
        blocks += [((a, 0), (a, tok_rows)) for a in three] + [((tok, 0), (grd, 0))]
    owners = [
        jnp.stack([((y * 2 + (zb ^ who)) * 2 + za) * local_count + n for n in range(local_count)]) for who in (0, 1)
    ]

    span = N_X * shard
    own_layout = [(j * N_C + k, 0, (j * N_C + k) * span, span) for j in range(N_ZH) for k in range(N_C)]
    near_layout = [
        (k, (i * N_ZH + j) * shard, (j * N_C + k) * span + i * shard, shard)
        for j in range(N_ZH)
        for k in range(N_C)
        for i in range(N_X)
    ]

    near_x, near_g, near_hid, near_slope, near_dots, near_at = inner(
        blocks, owners[1], near_weights, near_layout, hidden, SHORT
    )

    def scatter_x(both):
        return lax.psum_scatter(both, "dp", scatter_dimension=0, tiled=True, axis_index_groups=X_GROUPS)

    def at(j, i):
        return lambda k: (j * N_C + k) * N_X + i

    order = [at(j, i) for i in range(N_X) for j in range(N_ZH)]
    theirs = weight_grads(near_x, near_g, near_hid, near_slope, local_count, [n(1) for n in order], LONG)
    theirs = send(theirs, CORE)
    ours = weight_grads(near_x, near_g, near_hid, near_slope, local_count, [n(0) for n in order], LONG)
    near_sum = add(ours, theirs)

    following = send_ep(after(payload, near_hid), E_NEXT)
    far_rows, owners[0], near_sum, across, following = lax.optimization_barrier(
        (far_rows, owners[0], near_sum, across, following)
    )
    arrivals = [following, across, send_ep(across, E_PREV)]
    own_weights += [far_rows, send(far_rows, CORE)]
    near_grads = scatter_x(near_sum)
    own_x, own_g, own_hid, own_slope, own_dots, own_at = inner(
        blocks, owners[0], own_weights, own_layout, hidden, 1
    )
    theirs = weight_grads(own_x, own_g, own_hid, own_slope, local_count, [n(1) for n in order], 1)

    owners = jnp.concatenate(owners)

    def made(part, cost, *others):
        return outer(
            after(owners, *others),
            [own_at, near_at],
            [own_hid, near_hid],
            [own_slope, near_slope],
            [own_dots, near_dots],
            [own_weights, near_weights],
            [own_layout, near_layout],
            part,
            2,
            cost,
        )

    def halves(far_tok, far_rest):
        return send(far_tok, Y_UP), send(far_rest, Y_DOWN)

    mine_late, left, right, *far = made(1, LONG, theirs, *arrivals)
    far_late = halves(*far)
    own_sum = weight_grads(
        after(own_x, left),
        own_g,
        own_hid,
        own_slope,
        local_count,
        [n(0) for n in order],
        LONG,
        send(theirs, CORE),
    )
    own_sum, near_grads = lax.optimization_barrier((own_sum, near_grads))
    own_grads = scatter_x(own_sum)
    mine_soon, next_left, next_right, *next_far = made(0, LONG, own_sum)
    far_late, left, right, next_left, next_right, next_far, near_grads, place = lax.optimization_barrier(
        (far_late, left, right, next_left, next_right, next_far, near_grads, place)
    )
    near_grads = [near_grads[:shard], near_grads[shard:]]
    to_right = jnp.where(zb == 1, near_grads[1], near_grads[0])
    to_left = jnp.where(zb == 1, near_grads[0], near_grads[1])
    from_z = [send(to_right, Z_UP), send(to_left, Z_DOWN)]
    left, right = passed(left, right, *far_late)
    late = [mine_late, send(right, Y_UP), send(left, Y_DOWN)]
    next_far, next_left, next_right, late, from_z, own_grads, place = lax.optimization_barrier(
        (next_far, next_left, next_right, late, from_z, own_grads, hold(place))
    )
    from_z.append(send(own_grads[shard:], Z_FAR))
    other = functools.reduce(lambda a, b: a + b, [p.astype(F32) for p in late]).astype(BF16)
    from_pair = send(other, Z_PAIR)
    left, right = passed(next_left, next_right, *halves(*next_far))
    mixed, grad_tokens, table = total(place, mine_soon, send(right, Y_UP), send(left, Y_DOWN), from_pair)
    table = table[: 2 * experts // N_DP].reshape(2, experts, tok_rows)
    grad_probs = jnp.sum(jnp.where(hits, (table[0] + table[1])[:, None, :], 0.0), axis=0).T

    terms = [own_grads[:shard], *from_z]
    grad = functools.reduce(lambda a, b: a + b, [term.astype(F32) for term in terms])

    grads = [[grad[:, (s * local_count + n) * hidden :][:, :hidden] for n in range(local_count)] for s in (0, 1)]
    moved = migrate(leaving(grads).astype(BF16))
    arrived = jnp.where(ep == root, arrivals[0], jnp.where(ep == (root - 1) % N_EP, arrivals[1], arrivals[2]))
    mine = jnp.stack(mine).astype(jnp.int32)
    return (mixed, grad_tokens, grad_probs, *updates(mine, grad, moved, states, arrived))


def solution(mesh):
    tok = P(("ep", "dp"), None)
    gate, down = P("ep", "dp", None), P("ep", None, "dp")
    in_specs = (tok, tok, tok, tok, P(), P(), gate, gate, gate, down, down, down)
    out_specs = (tok, tok, tok, gate, gate, gate, down, down, down)
    return jax.shard_map(per_device, mesh=mesh, in_specs=in_specs, out_specs=out_specs, check_vma=False)
```

```python
import functools
import jax
import jax.numpy as jnp
from jax import lax
from jax.experimental import pallas as pl
from jax.experimental.pallas import tpu as pltpu
from jax.sharding import PartitionSpec as P

beta_one = 0.9
beta_two = 0.95
step_rate = 0.001
adam_eps = 1e-08

BOTH = ("ep", "dp")
N_Y, N_ZL, N_X, N_ZH, N_C = 4, 4, 4, 2, 2
N_EP, N_DP = N_Y * N_ZL, N_X * N_ZH * N_C
F32, BF16 = jnp.float32, jnp.bfloat16


def links(move):
    pairs = []
    for ep in range(N_EP):
        for dp in range(N_DP):
            y, zl = divmod(ep, N_ZL)
            x, rest = divmod(dp, N_ZH * N_C)
            zh, c = divmod(rest, N_C)
            y, x, z, c = move(y, x, zh * N_ZL + zl, c)
            zh, zl = divmod(z % (N_ZH * N_ZL), N_ZL)
            there = (y % N_Y * N_ZL + zl) * N_DP + x % N_X * N_ZH * N_C + zh * N_C + c
            pairs.append((ep * N_DP + dp, there))
    return pairs


Y_UP = links(lambda y, x, z, c: (y + 1, x, z, c))
Y_DOWN = links(lambda y, x, z, c: (y - 1, x, z, c))
X_UP = links(lambda y, x, z, c: (y, x + 1, z, c))
X_DOWN = links(lambda y, x, z, c: (y, x - 1, z, c))
Z_UP = links(lambda y, x, z, c: (y, x, z + 2, c))
Z_DOWN = links(lambda y, x, z, c: (y, x, z - 2, c))
Z_PAIR = links(lambda y, x, z, c: (y, x, z ^ 1, c))
Z_FAR = links(lambda y, x, z, c: (y, x, z + 4, c))
X_GROUPS = [[i * N_ZH * N_C + rest for i in range(N_X)] for rest in range(N_ZH * N_C)]
ROOM = 48
EXTRA = 16
VMEM = 56 * 2**20
SHORT, LONG = 10**9, 10**12
CORE = links(lambda y, x, z, c: (y, x, z, 1 - c))


E_NEXT = [(rank, (rank + 1) % N_EP) for rank in range(N_EP)]
E_HALF = [(rank, (rank + N_EP // 2) % N_EP) for rank in range(N_EP)]
E_PREV = [(rank, (rank - 1) % N_EP) for rank in range(N_EP)]


def after(array, *others):
    return lax.optimization_barrier((array, *others))[0]


def send(block, pairs):
    return lax.ppermute(block, BOTH, pairs)


def send_ep(block, pairs):
    return lax.ppermute(block, "ep", pairs)


def add(first, second):
    return (first.astype(F32) + second.astype(F32)).astype(BF16)


def adam_update(weight, first, second, grad):
    first_new = beta_one * first.astype(F32) + (1.0 - beta_one) * grad
    second_new = beta_two * second.astype(F32) + (1.0 - beta_two) * grad * grad
    weight_new = weight.astype(F32) - step_rate * first_new / (jnp.sqrt(second_new) + adam_eps)
    return weight_new.astype(BF16), first_new.astype(BF16), second_new.astype(BF16)


def updates(mine, grad, moved, states, arrived):
    local, shard, hidden = states[0].shape

    def body(mine_ref, grad_ref, moved_ref, *refs):
        ins, arrived_ref, outs = refs[:6], refs[6], refs[7:]
        for n in range(local):
            here = mine_ref[n] > 0
            for side in (0, 1):
                span = slice((side * local + n) * hidden, (side * local + n + 1) * hidden)
                value = jnp.where(here, moved_ref[:, side * hidden : (side + 1) * hidden].astype(F32), grad_ref[:, span])
                if side:
                    value = value.T
                state = []
                for kind in range(3):
                    column = (side * 3 + kind) * hidden
                    fresh = arrived_ref[:, column : column + hidden].astype(F32)
                    old = ins[side * 3 + kind][n].astype(F32)
                    state.append(jnp.where(here, fresh.T if side else fresh, old))
                for kind, done in enumerate(adam_update(*state, value)):
                    outs[side * 3 + kind][n] = done

    shapes = [jax.ShapeDtypeStruct(state.shape, BF16) for state in states]
    moved_bytes = 4 * 6 * local * shard * hidden
    return call(
        body, [SCALARS] + [NEAR] * 9, [(NEAR, shape) for shape in shapes], 0, moved_bytes
    )(mine, grad, moved, *states, arrived)


def dot(left, right, dims=((1,), (0,))):
    return lax.dot_general(left, right, (dims, ((), ())), preferred_element_type=F32)


COLS = ((1,), (1,))
ROWS = ((0,), (0,))
NEAR = pl.BlockSpec(memory_space=pltpu.VMEM)
AWAY = pl.BlockSpec(memory_space=pl.ANY)
SCALARS = pl.BlockSpec(memory_space=pltpu.SMEM)


def call(body, ins, outs, flops, moved, scratch=(), grid=()):
    return pl.pallas_call(
        body,
        grid=grid,
        in_specs=list(ins),
        out_specs=[spec for spec, _ in outs],
        out_shape=[shape for _, shape in outs],
        scratch_shapes=list(scratch),
        compiler_params=pltpu.CompilerParams(vmem_limit_bytes=VMEM),
        cost_estimate=pl.CostEstimate(flops=flops, bytes_accessed=moved, transcendentals=0),
    )


def relative(n, zh, c):
    j, k, i = n // (N_C * N_X), n // N_X % N_C, n % N_X
    return (i * N_ZH + (j ^ zh)) * N_C + (k ^ c)


def pack(place, tokens, grads, table):
    rows, width = tokens.shape
    block = width // N_DP

    def body(place_ref, tok_ref, grd_ref, table_ref, out_ref):
        zh, c = place_ref[0], place_ref[1]
        for n in range(N_DP):
            at = pl.multiple_of(relative(n, zh, c) * block, block)
            here = slice(n * block, (n + 1) * block)
            out_ref[:rows, here] = tok_ref[:, pl.ds(at, block)]
            out_ref[rows : 2 * rows, here] = grd_ref[:, pl.ds(at, block)]
        out_ref[2 * rows :, :] = table_ref[...]

    shape = jax.ShapeDtypeStruct((2 * rows + EXTRA, width), BF16)
    return call(body, [SCALARS] + [NEAR] * 3, [(NEAR, shape)], 0, 8 * rows * width)(place, tokens, grads, table)[0]


def total(place, *arrays):
    rows, width = arrays[0].shape
    rows = (rows - EXTRA) // 2
    block = width // N_DP

    def body(place_ref, *refs):
        zh, c = place_ref[0], place_ref[1]
        ins, (mixed_ref, back_ref, table_ref) = refs[:-3], refs[-3:]

        def added(at, here):
            value = ins[0][at, here].astype(F32)
            for source in ins[1:]:
                value = value + source[at, here].astype(F32)
            return value

        for n in range(N_DP):
            at = pl.multiple_of(relative(n, zh, c) * block, block)
            here = slice(n * block, (n + 1) * block)
            mixed_ref[:, pl.ds(at, block)] = added(slice(0, rows), here).astype(BF16)
            back_ref[:, pl.ds(at, block)] = added(slice(rows, 2 * rows), here).astype(BF16)
        table_ref[...] = added(slice(2 * rows, 2 * rows + EXTRA), slice(0, width))

    outs = [(NEAR, jax.ShapeDtypeStruct((rows, width), BF16))] * 2
    outs.append((NEAR, jax.ShapeDtypeStruct((EXTRA, width), F32)))
    return call(body, [SCALARS] + [NEAR] * len(arrays), outs, 0, 20 * rows * width)(place, *arrays)


def hold(place):
    def body(place_ref, out_ref):
        for n in range(2):
            out_ref[n] = place_ref[n]

    return call(body, [SCALARS], [(SCALARS, jax.ShapeDtypeStruct(place.shape, place.dtype))], 2**40, 0)(place)[0]


def passed(left, right, from_left, from_right):
    size = from_left.shape[0]
    width = left.shape[1]

    def body(left_ref, right_ref, from_left_ref, from_right_ref, left_out, right_out):
        left_out[:size] = left_ref[:size]
        left_out[size:] = add(left_ref[size:], from_right_ref[...])
        right_out[:size] = add(right_ref[:size], from_left_ref[...])
        right_out[size:] = right_ref[size:]

    tile = width // 4
    down = lambda array: pl.BlockSpec((array.shape[0], tile), lambda i: (0, i))
    arrays = (left, right, from_left, from_right)
    shape = jax.ShapeDtypeStruct(left.shape, BF16)
    return call(body, [down(a) for a in arrays], [(down(left), shape)] * 2, 0, 0, (), (4,))(*arrays)


def chosen(at, rows):
    return lax.broadcasted_iota(jnp.int32, (rows, at.shape[1]), 0).astype(F32) == at


def inner(blocks, owners, weights, layout, hidden, cost):
    count = len(blocks)
    size, width = blocks[0][0][0].shape[1] // N_DP, blocks[0][0][0].shape[1]
    local = owners.shape[0]
    cut = local * hidden
    rows = count * ROOM
    arrays = []
    for block in blocks:
        for array, _ in block:
            if not any(array is other for other in arrays):
                arrays.append(array)
    index = lambda array: next(n for n, other in enumerate(arrays) if other is array)
    starts = [[(index(array), start) for array, start in block] for block in blocks]
    spans = [(side * local + n) * hidden for n in range(local) for side in (0, 1)]

    def body(owner_ref, *refs):
        sources, stored = refs[: len(arrays)], refs[len(arrays) : len(arrays) + len(weights)]
        x_ref, g_ref, hid_ref, slope_ref, dots_ref, at_ref, held, tables, weight, sem, weight_sem = refs[
            len(arrays) + len(weights) :
        ]
        moves, fills = [], []
        for b, block in enumerate(starts):
            moves.append(
                [
                    pltpu.make_async_copy(
                        sources[which].at[pl.ds(start, size), :],
                        held.at[b, pl.ds(side * size, size), :],
                        sem.at[2 * b + side],
                    )
                    for side, (which, start) in enumerate(block)
                ]
            )
            which, start = block[1]
            moves[b].append(
                pltpu.make_async_copy(
                    sources[which].at[pl.ds(start + size, EXTRA), :], tables.at[b], sem.at[2 * count + b]
                )
            )
        for number, span in enumerate(spans):
            fills.append(
                [
                    pltpu.make_async_copy(
                        stored[which].at[pl.ds(start, depth), pl.ds(span, hidden)],
                        weight.at[pl.ds(to, depth), pl.ds(span, hidden)],
                        weight_sem.at[number * len(layout) + entry],
                    )
                    for entry, (which, start, to, depth) in enumerate(layout)
                ]
            )
        for group in moves + fills:
            for copy in group:
                copy.start()
        factors = [[] for _ in range(local)]
        lines = lax.broadcasted_iota(jnp.int32, (EXTRA, size), 0)
        for b in range(count):
            for copy in moves[b]:
                copy.wait()
            hits = []
            for n in range(local):
                slot = owner_ref[n]
                lanes = pl.ds(pl.multiple_of(slot % N_DP * size, size), size)
                tile = tables[b, :, lanes].astype(F32)
                line = slot // N_DP
                entry = lambda kind: jnp.sum(jnp.where(lines == line + 2 * kind, tile, 0.0), axis=0, keepdims=True)
                number = entry(0)
                at_ref[b * local + n : b * local + n + 1, :] = number
                hits.append(chosen(number, ROOM))
                factors[n].append(jnp.sum(jnp.where(hits[n], entry(1) + entry(2), 0.0), axis=1, keepdims=True))
            pick = jnp.concatenate([hit.astype(F32) for hit in hits], axis=0).astype(BF16)
            for side, target in enumerate((x_ref, g_ref)):
                got = dot(pick, held[b, side * size : (side + 1) * size, :]).astype(BF16)
                for n in range(local):
                    target[n * rows + b * ROOM : n * rows + (b + 1) * ROOM, :] = got[n * ROOM : (n + 1) * ROOM]
        for n in range(local):
            for copy in fills[2 * n] + fills[2 * n + 1]:
                copy.wait()
            mine = slice(n * rows, (n + 1) * rows)
            here = dot(x_ref[mine, :], weight[:, n * hidden : (n + 1) * hidden])
            over = dot(g_ref[mine, :], weight[:, cut + n * hidden : cut + (n + 1) * hidden])
            factor = jnp.concatenate(factors[n], axis=0)
            sigmoid = jax.nn.sigmoid(here)
            act = here * sigmoid
            hid_ref[mine, :] = (factor * act).astype(BF16)
            slope_ref[mine, :] = (factor * over * (sigmoid + act * (1.0 - sigmoid))).astype(BF16)
            sums = jnp.sum(act * over, axis=1, keepdims=True)
            for b in range(count):
                hit = chosen(at_ref[b * local + n : b * local + n + 1, :], ROOM)
                spread = jnp.where(hit, sums[b * ROOM : (b + 1) * ROOM], 0.0)
                dots_ref[b * local + n : b * local + n + 1, :] = jnp.sum(spread, axis=0, keepdims=True)

    shape = lambda last, kind: jax.ShapeDtypeStruct((local * rows, last), kind)
    outs = [(NEAR, shape(width, BF16))] * 2 + [(NEAR, shape(hidden, BF16))] * 2
    outs += [(NEAR, jax.ShapeDtypeStruct((count * local, size), F32))] * 2
    return call(
        body,
        [SCALARS] + [AWAY] * (len(arrays) + len(weights)),
        outs,
        cost,
        1,
        [
            pltpu.VMEM((count, 2 * size, width), BF16),
            pltpu.VMEM((count, EXTRA, width), BF16),
            pltpu.VMEM((width, 2 * cut), BF16),
            pltpu.SemaphoreType.DMA((3 * count,)),
            pltpu.SemaphoreType.DMA((len(spans) * len(layout),)),
        ],
    )(owners, *arrays, *weights)


def outer(owners, ats, hids, slopes, dots, weights, layouts, part, parts, cost):
    ranks = len(hids)
    size = ats[0].shape[1]
    local = owners.shape[0] // ranks
    hidden = hids[0].shape[1]
    cut = local * hidden
    every = hids[0].shape[0] // local
    rows = every // parts
    blocks = rows // ROOM
    width = size * N_DP
    steps = N_ZH * N_C
    depth = width // steps
    counts = [len(some) for some in weights]
    tall = 2 * size + EXTRA

    def target(outs, b, piece):
        if b < blocks - 1:
            return outs[b], piece * size
        return (outs[b], 0) if piece == 0 else (outs[b + 1], (piece - 1) * size)

    def body(owner_ref, *refs):
        at_refs, refs = refs[:ranks], refs[ranks:]
        hid_refs, refs = refs[:ranks], refs[ranks:]
        slope_refs, refs = refs[:ranks], refs[ranks:]
        dots_refs, refs = refs[:ranks], refs[ranks:]
        flat, outs, (first, second, sem) = refs[: sum(counts)], refs[sum(counts) : -3], refs[-3:]
        sources = [flat[: counts[0]], flat[counts[0] :]]
        held = [first, second]
        fills = [[] for _ in range(steps)]
        number = 0
        for step in range(steps):
            for who in range(ranks):
                for which, start, to, many in layouts[who]:
                    if to // depth == step:
                        fills[step].append(
                            pltpu.make_async_copy(
                                sources[who][which].at[pl.ds(start, many), :],
                                held[who].at[pl.ds(to, many), :],
                                sem.at[number],
                            )
                        )
                        number += 1
        for group in fills:
            for copy in group:
                copy.start()
        picks = []
        for b in range(blocks):
            hits = []
            for who in range(ranks):
                for n in range(local):
                    row = (part * blocks + b) * local + n
                    hits.append(chosen(at_refs[who][row : row + 1, :], ROOM).astype(F32))
            picks.append(jnp.concatenate(hits, axis=0).astype(BF16))
        lines = lax.broadcasted_iota(jnp.int32, (EXTRA, size), 0)
        for b in range(blocks):
            values = []
            for who in range(ranks):
                for n in range(local):
                    row = (part * blocks + b) * local + n
                    value = dots_refs[who][row : row + 1, :]
                    high = value.astype(BF16).astype(F32)
                    values.append((owner_ref[who * local + n], high, value - high))
            for lane in range(N_DP):
                tile = jnp.zeros((EXTRA, size), F32)
                for slot, high, low in values:
                    line = jnp.where(slot % N_DP == lane, slot // N_DP, EXTRA)
                    tile = jnp.where(lines == line, high, tile)
                    tile = jnp.where(lines == line + 2, low, tile)
                out_ref, begin = target(outs, b, 2)
                out_ref[begin : begin + EXTRA, lane * size : (lane + 1) * size] = tile.astype(BF16)
        for step in range(steps):
            for copy in fills[step]:
                copy.wait()
            span = slice(step * depth, (step + 1) * depth)
            for side in (0, 1):
                made = []
                for who in range(ranks):
                    for n in range(local):
                        begin = n * every + part * rows
                        left = (hid_refs, slope_refs)[side][who][begin : begin + rows, :]
                        column = ((1 - side) * local + n) * hidden
                        made.append(dot(left, held[who][span, column : column + hidden], COLS).astype(BF16))
                for b in range(blocks):
                    stack = jnp.concatenate([m[b * ROOM : (b + 1) * ROOM] for m in made], axis=0)
                    out_ref, begin = target(outs, b, side)
                    out_ref[begin : begin + size, span] = dot(picks[b], stack, ROWS).astype(BF16)

    entries = sum(len(layout) for layout in layouts)
    return call(
        body,
        [SCALARS] + [NEAR] * (4 * ranks) + [AWAY] * sum(counts),
        [
            (NEAR, jax.ShapeDtypeStruct((many, width), BF16))
            for many in [tall] * (blocks - 1) + [size, tall - size]
        ],
        cost,
        1,
        [pltpu.VMEM((width, 2 * cut), BF16)] * 2 + [pltpu.SemaphoreType.DMA((entries,))],
    )(owners, *ats, *hids, *slopes, *dots, *[w for some in weights for w in some])


def weight_grads(toks, grds, hid, slope, local, order, cost, theirs=None):
    tall, width = toks.shape
    hidden = hid.shape[1]
    rows = tall // local
    size = width // N_DP
    group = 4
    steps = len(order) // group

    def body(*refs):
        ins, (hid_ref, slope_ref, *theirs_ref, out_ref) = refs[: 2 * group], refs[2 * group :]
        for side, other in ((0, slope_ref), (1, hid_ref)):
            these = ins[side * group : (side + 1) * group]
            for n in range(local):
                mine = slice(n * rows, (n + 1) * rows)
                left = jnp.concatenate([r[mine, :] for r in these], axis=1)
                span = slice((side * local + n) * hidden, (side * local + n + 1) * hidden)
                value = dot(left, other[mine, :], ROWS)
                for more in theirs_ref:
                    value = value + more[:, span].astype(F32)
                out_ref[:, span] = value.astype(BF16)

    def spec(n):
        places = [order[step * group + n] for step in range(steps)]

        def index(i):
            here = places[0]
            for step in range(1, steps):
                here = jnp.where(i == step, places[step], here)
            return (0, here)

        return pl.BlockSpec((tall, size), index)

    whole = pl.BlockSpec(hid.shape, lambda i: (0, 0), pipeline_mode=pl.Buffered(1))
    out = pl.BlockSpec((group * size, 2 * local * hidden), lambda i: (i, 0))
    extra = [] if theirs is None else [theirs]
    return call(
        body,
        [spec(n) for n in range(group)] * 2 + [whole, whole] + [out] * len(extra),
        [(out, jax.ShapeDtypeStruct((len(order) * size, 2 * local * hidden), BF16))],
        cost,
        1,
        (),
        (steps,),
    )(*[toks] * group, *[grds] * group, hid, slope, *extra)[0]


def per_device(tokens, grad_out, routes, probs, old_place, new_place, gate_w, gate_m, gate_v, down_w, down_m, down_v):
    tok_rows, width = tokens.shape
    experts = old_place.shape[0]
    local_count, shard, hidden = gate_w.shape
    ep, dp = lax.axis_index("ep"), lax.axis_index("dp")
    y, zl = ep // N_ZL, ep % N_ZL
    zb, za = zl // 2, zl % 2
    zh, c = dp // N_C % N_ZH, dp % N_C
    slots = jnp.arange(experts, dtype=jnp.int32)
    place = jnp.stack([zh, c]).astype(jnp.int32)

    inverse = jnp.sum(jnp.where(old_place[None, :] == slots[:, None], slots[None, :], 0), axis=1)
    slot = jnp.sum(jnp.where(routes[:, :, None] == slots, inverse, 0), axis=2)
    hits = slot.T[None] == slots[:, None, None]
    by_slot = jnp.sum(jnp.where(hits, probs.T[None], 0.0), axis=1)
    named = jnp.any(hits, axis=1)
    before = jnp.arange(tok_rows)[:, None] < jnp.arange(tok_rows)[None, :]
    number = jnp.where(named, dot(named.astype(BF16), before.astype(BF16)), -1.0)
    high = by_slot.astype(BF16)
    low = (by_slot - high.astype(F32)).astype(BF16)
    table = jnp.concatenate([number.astype(BF16), high, low], axis=0).reshape(-1, width)
    table = jnp.pad(table, ((0, EXTRA - table.shape[0]), (0, 0)))
    here = pack(place, tokens, grad_out, table)

    def side(state):
        return jnp.transpose(state, (0, 2, 1))

    weights = [gate_w, side(down_w)]
    block = jnp.concatenate([state[n] for state in weights for n in range(local_count)], axis=1)

    def gather_x(rows):
        return lax.all_gather(rows, "dp", axis=0, tiled=True, axis_index_groups=X_GROUPS)

    changed = new_place != old_place
    source = jnp.sum(jnp.where(new_place[:, None] == old_place[None, :], slots[None, :], 0), axis=1)
    first = changed & (source // local_count == (slots // local_count - 1) % N_EP)
    root = jnp.sum(jnp.where(first, slots // local_count, 0))
    mine = [jnp.any(changed & (slots == ep * local_count + n)) for n in range(local_count)]

    def migrate(payload):
        def branch(rank):
            stops = [(rank - 1) % N_EP, rank, (rank - 1 - N_EP // 2) % N_EP, (rank - 1) % N_EP]
            pairs = [(stops[0], stops[1]), (stops[2], stops[3]), (stops[1], stops[2])]
            return lambda part: lax.ppermute(part, "ep", pairs)

        return lax.switch(root, [branch(rank) for rank in range(N_EP)], payload)

    def leaving(states):
        return jnp.concatenate([jnp.where(mine[1], state[1], state[0]) for state in states], axis=1)

    states = [gate_w, gate_m, gate_v, down_w, down_m, down_v]
    payload = leaving([gate_w, gate_m, gate_v] + [side(state) for state in states[3:]])

    own_rows = gather_x(block)
    block = after(block, here)
    z_left, z_right = send(block, Z_UP), send(block, Z_DOWN)
    up, down = send(here, Y_UP), send(here, Y_DOWN)
    z_left, z_right, up, down, here, block, own_rows, payload = lax.optimization_barrier(
        (z_left, z_right, up, down, here, block, own_rows, payload)
    )
    near = jnp.concatenate([jnp.where(zb == 1, z_left, z_right), jnp.where(zb == 1, z_right, z_left)], axis=0)
    near_rows = gather_x(near)
    pair = send(here, Z_PAIR)
    far_tok, far_grd = send(up[:tok_rows], Y_UP), send(down[tok_rows:], Y_DOWN)
    pair, far_tok, far_grd, block = lax.optimization_barrier((pair, far_tok, far_grd, block))
    pair_up, pair_down = send(pair, Y_UP), send(pair, Y_DOWN)
    far = send(block, Z_FAR)
    pair_up, pair_down, far, near_rows = lax.optimization_barrier((pair_up, pair_down, far, near_rows))
    pair_far_tok, pair_far_grd = send(pair_up[:tok_rows], Y_UP), send(pair_down[tok_rows:], Y_DOWN)
    far_rows = gather_x(far)
    near_weights = [near_rows, send(near_rows, CORE)]
    own_weights = [own_rows, send(own_rows, CORE)]
    blocks = []
    for three, tok, grd in (
        ((here, up, down), far_tok, far_grd),
        ((pair, pair_up, pair_down), pair_far_tok, pair_far_grd),
    ):
        blocks += [((a, 0), (a, tok_rows)) for a in three] + [((tok, 0), (grd, 0))]
    owners = [
        jnp.stack([((y * 2 + (zb ^ who)) * 2 + za) * local_count + n for n in range(local_count)]) for who in (0, 1)
    ]

    span = N_X * shard
    own_layout = [(j * N_C + k, 0, (j * N_C + k) * span, span) for j in range(N_ZH) for k in range(N_C)]
    near_layout = [
        (k, (i * N_ZH + j) * shard, (j * N_C + k) * span + i * shard, shard)
        for j in range(N_ZH)
        for k in range(N_C)
        for i in range(N_X)
    ]

    near_x, near_g, near_hid, near_slope, near_dots, near_at = inner(
        blocks, owners[1], near_weights, near_layout, hidden, SHORT
    )

    def scatter_x(both):
        return lax.psum_scatter(both, "dp", scatter_dimension=0, tiled=True, axis_index_groups=X_GROUPS)

    def at(j, i):
        return lambda k: (j * N_C + k) * N_X + i

    order = [at(j, i) for i in range(N_X) for j in range(N_ZH)]
    theirs = weight_grads(near_x, near_g, near_hid, near_slope, local_count, [n(1) for n in order], LONG)
    theirs = send(theirs, CORE)
    ours = weight_grads(near_x, near_g, near_hid, near_slope, local_count, [n(0) for n in order], LONG)
    near_sum = add(ours, theirs)

    payload = after(payload, near_hid)
    across, following = send_ep(payload, E_HALF), send_ep(payload, E_NEXT)
    far_rows, owners[0], near_sum, across, following = lax.optimization_barrier(
        (far_rows, owners[0], near_sum, across, following)
    )
    arrivals = [following, across, send_ep(across, E_PREV)]
    own_weights += [far_rows, send(far_rows, CORE)]
    near_grads = scatter_x(near_sum)
    own_x, own_g, own_hid, own_slope, own_dots, own_at = inner(
        blocks, owners[0], own_weights, own_layout, hidden, 1
    )
    theirs = weight_grads(own_x, own_g, own_hid, own_slope, local_count, [n(1) for n in order], 1)

    owners = jnp.concatenate(owners)

    def made(part, cost, *others):
        return outer(
            after(owners, *others),
            [own_at, near_at],
            [own_hid, near_hid],
            [own_slope, near_slope],
            [own_dots, near_dots],
            [own_weights, near_weights],
            [own_layout, near_layout],
            part,
            2,
            cost,
        )

    def halves(far_tok, far_rest):
        return send(far_tok, Y_UP), send(far_rest, Y_DOWN)

    mine_late, left, right, *far = made(1, LONG, theirs, *arrivals)
    far_late = halves(*far)
    own_sum = weight_grads(
        after(own_x, left),
        own_g,
        own_hid,
        own_slope,
        local_count,
        [n(0) for n in order],
        LONG,
        send(theirs, CORE),
    )
    own_sum, near_grads, far_late, left, right = lax.optimization_barrier(
        (own_sum, near_grads, far_late, left, right)
    )
    own_grads = scatter_x(own_sum)
    left, right = passed(left, right, *far_late)
    late = [mine_late, send(right, Y_UP), send(left, Y_DOWN)]
    near_grads = [near_grads[:shard], near_grads[shard:]]
    to_right = jnp.where(zb == 1, near_grads[1], near_grads[0])
    to_left = jnp.where(zb == 1, near_grads[0], near_grads[1])
    from_z = [send(to_right, Z_UP), send(to_left, Z_DOWN)]
    mine_soon, next_left, next_right, *next_far = made(0, LONG, own_sum, left, right, to_right, to_left)
    next_far, from_z, place = lax.optimization_barrier((next_far, from_z, place))
    far_soon, place = lax.optimization_barrier((halves(*next_far), hold(place)))
    left, right = passed(next_left, next_right, *far_soon)
    soon = [mine_soon, send(right, Y_UP), send(left, Y_DOWN)]
    other = functools.reduce(lambda a, b: a + b, [p.astype(F32) for p in late]).astype(BF16)
    from_pair, own_grads, place = lax.optimization_barrier(
        (send(other, Z_PAIR), own_grads, hold(after(place, left, right, other)))
    )
    from_far, place = lax.optimization_barrier((send(own_grads[shard:], Z_FAR), place))
    from_z.append(from_far)
    mixed, grad_tokens, table = total(place, *soon, from_pair)
    table = table[: 2 * experts // N_DP].reshape(2, experts, tok_rows)
    grad_probs = jnp.sum(jnp.where(hits, (table[0] + table[1])[:, None, :], 0.0), axis=0).T

    terms = [own_grads[:shard], *from_z]
    grad = functools.reduce(lambda a, b: a + b, [term.astype(F32) for term in terms])

    grads = [[grad[:, (s * local_count + n) * hidden :][:, :hidden] for n in range(local_count)] for s in (0, 1)]
    moved = migrate(leaving(grads).astype(BF16))
    arrived = jnp.where(ep == root, arrivals[0], jnp.where(ep == (root - 1) % N_EP, arrivals[1], arrivals[2]))
    mine = jnp.stack(mine).astype(jnp.int32)
    return (mixed, grad_tokens, grad_probs, *updates(mine, grad, moved, states, arrived))


def solution(mesh):
    tok = P(("ep", "dp"), None)
    gate, down = P("ep", "dp", None), P("ep", None, "dp")
    in_specs = (tok, tok, tok, tok, P(), P(), gate, gate, gate, down, down, down)
    out_specs = (tok, tok, tok, gate, gate, gate, down, down, down)
    return jax.shard_map(per_device, mesh=mesh, in_specs=in_specs, out_specs=out_specs, check_vma=False)
```

```python
import functools
import jax
import jax.numpy as jnp
from jax import lax
from jax.experimental import pallas as pl
from jax.experimental.pallas import tpu as pltpu
from jax.sharding import PartitionSpec as P

beta_one = 0.9
beta_two = 0.95
step_rate = 0.001
adam_eps = 1e-08

BOTH = ("ep", "dp")
N_Y, N_ZL, N_X, N_ZH, N_C = 4, 4, 4, 2, 2
N_EP, N_DP = N_Y * N_ZL, N_X * N_ZH * N_C
F32, BF16 = jnp.float32, jnp.bfloat16


def links(move):
    pairs = []
    for ep in range(N_EP):
        for dp in range(N_DP):
            y, zl = divmod(ep, N_ZL)
            x, rest = divmod(dp, N_ZH * N_C)
            zh, c = divmod(rest, N_C)
            y, x, z, c = move(y, x, zh * N_ZL + zl, c)
            zh, zl = divmod(z % (N_ZH * N_ZL), N_ZL)
            there = (y % N_Y * N_ZL + zl) * N_DP + x % N_X * N_ZH * N_C + zh * N_C + c
            pairs.append((ep * N_DP + dp, there))
    return pairs


Y_UP = links(lambda y, x, z, c: (y + 1, x, z, c))
Y_DOWN = links(lambda y, x, z, c: (y - 1, x, z, c))
X_UP = links(lambda y, x, z, c: (y, x + 1, z, c))
X_DOWN = links(lambda y, x, z, c: (y, x - 1, z, c))
Z_UP = links(lambda y, x, z, c: (y, x, z + 2, c))
Z_DOWN = links(lambda y, x, z, c: (y, x, z - 2, c))
Z_PAIR = links(lambda y, x, z, c: (y, x, z ^ 1, c))
Z_FAR = links(lambda y, x, z, c: (y, x, z + 4, c))
X_GROUPS = [[i * N_ZH * N_C + rest for i in range(N_X)] for rest in range(N_ZH * N_C)]
ROOM = 48
EXTRA = 16
VMEM = 56 * 2**20
SHORT, LONG = 10**9, 10**12
CORE = links(lambda y, x, z, c: (y, x, z, 1 - c))


E_NEXT = [(rank, (rank + 1) % N_EP) for rank in range(N_EP)]
E_HALF = [(rank, (rank + N_EP // 2) % N_EP) for rank in range(N_EP)]
E_PREV = [(rank, (rank - 1) % N_EP) for rank in range(N_EP)]


def after(array, *others):
    return lax.optimization_barrier((array, *others))[0]


def send(block, pairs):
    return lax.ppermute(block, BOTH, pairs)


def send_ep(block, pairs):
    return lax.ppermute(block, "ep", pairs)


def add(first, second):
    return (first.astype(F32) + second.astype(F32)).astype(BF16)


def adam_update(weight, first, second, grad):
    first_new = beta_one * first.astype(F32) + (1.0 - beta_one) * grad
    second_new = beta_two * second.astype(F32) + (1.0 - beta_two) * grad * grad
    weight_new = weight.astype(F32) - step_rate * first_new / (jnp.sqrt(second_new) + adam_eps)
    return weight_new.astype(BF16), first_new.astype(BF16), second_new.astype(BF16)


def updates(mine, grad, moved, states, arrived):
    local, shard, hidden = states[0].shape

    def body(mine_ref, grad_ref, moved_ref, *refs):
        ins, arrived_ref, outs = refs[:6], refs[6], refs[7:]
        for n in range(local):
            here = mine_ref[n] > 0
            for side in (0, 1):
                span = slice((side * local + n) * hidden, (side * local + n + 1) * hidden)
                value = jnp.where(here, moved_ref[:, side * hidden : (side + 1) * hidden].astype(F32), grad_ref[:, span])
                if side:
                    value = value.T
                state = []
                for kind in range(3):
                    column = (side * 3 + kind) * hidden
                    fresh = arrived_ref[:, column : column + hidden].astype(F32)
                    old = ins[side * 3 + kind][n].astype(F32)
                    state.append(jnp.where(here, fresh.T if side else fresh, old))
                for kind, done in enumerate(adam_update(*state, value)):
                    outs[side * 3 + kind][n] = done

    shapes = [jax.ShapeDtypeStruct(state.shape, BF16) for state in states]
    moved_bytes = 4 * 6 * local * shard * hidden
    return call(
        body, [SCALARS] + [NEAR] * 9, [(NEAR, shape) for shape in shapes], 0, moved_bytes
    )(mine, grad, moved, *states, arrived)


def dot(left, right, dims=((1,), (0,))):
    return lax.dot_general(left, right, (dims, ((), ())), preferred_element_type=F32)


COLS = ((1,), (1,))
ROWS = ((0,), (0,))
NEAR = pl.BlockSpec(memory_space=pltpu.VMEM)
AWAY = pl.BlockSpec(memory_space=pl.ANY)
SCALARS = pl.BlockSpec(memory_space=pltpu.SMEM)


def call(body, ins, outs, flops, moved, scratch=(), grid=()):
    return pl.pallas_call(
        body,
        grid=grid,
        in_specs=list(ins),
        out_specs=[spec for spec, _ in outs],
        out_shape=[shape for _, shape in outs],
        scratch_shapes=list(scratch),
        compiler_params=pltpu.CompilerParams(vmem_limit_bytes=VMEM),
        cost_estimate=pl.CostEstimate(flops=flops, bytes_accessed=moved, transcendentals=0),
    )


def relative(n, zh, c):
    j, k, i = n // (N_C * N_X), n // N_X % N_C, n % N_X
    return (i * N_ZH + (j ^ zh)) * N_C + (k ^ c)


def pack(place, tokens, grads, table):
    rows, width = tokens.shape
    block = width // N_DP

    def body(place_ref, tok_ref, grd_ref, table_ref, out_ref):
        zh, c = place_ref[0], place_ref[1]
        for n in range(N_DP):
            at = pl.multiple_of(relative(n, zh, c) * block, block)
            here = slice(n * block, (n + 1) * block)
            out_ref[:rows, here] = tok_ref[:, pl.ds(at, block)]
            out_ref[rows : 2 * rows, here] = grd_ref[:, pl.ds(at, block)]
        out_ref[2 * rows :, :] = table_ref[...]

    shape = jax.ShapeDtypeStruct((2 * rows + EXTRA, width), BF16)
    return call(body, [SCALARS] + [NEAR] * 3, [(NEAR, shape)], 0, 8 * rows * width)(place, tokens, grads, table)[0]


def total(place, *arrays):
    rows, width = arrays[0].shape
    rows = (rows - EXTRA) // 2
    block = width // N_DP

    def body(place_ref, *refs):
        zh, c = place_ref[0], place_ref[1]
        ins, (mixed_ref, back_ref, table_ref) = refs[:-3], refs[-3:]

        def added(at, here):
            value = ins[0][at, here].astype(F32)
            for source in ins[1:]:
                value = value + source[at, here].astype(F32)
            return value

        for n in range(N_DP):
            at = pl.multiple_of(relative(n, zh, c) * block, block)
            here = slice(n * block, (n + 1) * block)
            mixed_ref[:, pl.ds(at, block)] = added(slice(0, rows), here).astype(BF16)
            back_ref[:, pl.ds(at, block)] = added(slice(rows, 2 * rows), here).astype(BF16)
        table_ref[...] = added(slice(2 * rows, 2 * rows + EXTRA), slice(0, width))

    outs = [(NEAR, jax.ShapeDtypeStruct((rows, width), BF16))] * 2
    outs.append((NEAR, jax.ShapeDtypeStruct((EXTRA, width), F32)))
    return call(body, [SCALARS] + [NEAR] * len(arrays), outs, 0, 20 * rows * width)(place, *arrays)


def hold(place):
    def body(place_ref, out_ref):
        for n in range(2):
            out_ref[n] = place_ref[n]

    return call(body, [SCALARS], [(SCALARS, jax.ShapeDtypeStruct(place.shape, place.dtype))], 2**40, 0)(place)[0]


def passed(left, right, from_left, from_right):
    size = from_left.shape[0]
    width = left.shape[1]

    def body(left_ref, right_ref, from_left_ref, from_right_ref, left_out, right_out):
        left_out[:size] = left_ref[:size]
        left_out[size:] = add(left_ref[size:], from_right_ref[...])
        right_out[:size] = add(right_ref[:size], from_left_ref[...])
        right_out[size:] = right_ref[size:]

    tile = width // 4
    down = lambda array: pl.BlockSpec((array.shape[0], tile), lambda i: (0, i))
    arrays = (left, right, from_left, from_right)
    shape = jax.ShapeDtypeStruct(left.shape, BF16)
    return call(body, [down(a) for a in arrays], [(down(left), shape)] * 2, 0, 0, (), (4,))(*arrays)


def chosen(at, rows):
    return lax.broadcasted_iota(jnp.int32, (rows, at.shape[1]), 0).astype(F32) == at


def inner(blocks, owners, weights, layout, hidden, cost):
    count = len(blocks)
    size, width = blocks[0][0][0].shape[1] // N_DP, blocks[0][0][0].shape[1]
    local = owners.shape[0]
    cut = local * hidden
    rows = count * ROOM
    arrays = []
    for block in blocks:
        for array, _ in block:
            if not any(array is other for other in arrays):
                arrays.append(array)
    index = lambda array: next(n for n, other in enumerate(arrays) if other is array)
    starts = [[(index(array), start) for array, start in block] for block in blocks]
    spans = [(side * local + n) * hidden for n in range(local) for side in (0, 1)]

    def body(owner_ref, *refs):
        sources, stored = refs[: len(arrays)], refs[len(arrays) : len(arrays) + len(weights)]
        x_ref, g_ref, hid_ref, slope_ref, dots_ref, at_ref, held, tables, weight, sem, weight_sem = refs[
            len(arrays) + len(weights) :
        ]
        moves, fills = [], []
        for b, block in enumerate(starts):
            moves.append(
                [
                    pltpu.make_async_copy(
                        sources[which].at[pl.ds(start, size), :],
                        held.at[b, pl.ds(side * size, size), :],
                        sem.at[2 * b + side],
                    )
                    for side, (which, start) in enumerate(block)
                ]
            )
            which, start = block[1]
            moves[b].append(
                pltpu.make_async_copy(
                    sources[which].at[pl.ds(start + size, EXTRA), :], tables.at[b], sem.at[2 * count + b]
                )
            )
        for number, span in enumerate(spans):
            fills.append(
                [
                    pltpu.make_async_copy(
                        stored[which].at[pl.ds(start, depth), pl.ds(span, hidden)],
                        weight.at[pl.ds(to, depth), pl.ds(span, hidden)],
                        weight_sem.at[number * len(layout) + entry],
                    )
                    for entry, (which, start, to, depth) in enumerate(layout)
                ]
            )
        for group in moves + fills:
            for copy in group:
                copy.start()
        factors = [[] for _ in range(local)]
        lines = lax.broadcasted_iota(jnp.int32, (EXTRA, size), 0)
        for b in range(count):
            for copy in moves[b]:
                copy.wait()
            hits = []
            for n in range(local):
                slot = owner_ref[n]
                lanes = pl.ds(pl.multiple_of(slot % N_DP * size, size), size)
                tile = tables[b, :, lanes].astype(F32)
                line = slot // N_DP
                entry = lambda kind: jnp.sum(jnp.where(lines == line + 2 * kind, tile, 0.0), axis=0, keepdims=True)
                number = entry(0)
                at_ref[b * local + n : b * local + n + 1, :] = number
                hits.append(chosen(number, ROOM))
                factors[n].append(jnp.sum(jnp.where(hits[n], entry(1) + entry(2), 0.0), axis=1, keepdims=True))
            pick = jnp.concatenate([hit.astype(F32) for hit in hits], axis=0).astype(BF16)
            for side, target in enumerate((x_ref, g_ref)):
                got = dot(pick, held[b, side * size : (side + 1) * size, :]).astype(BF16)
                for n in range(local):
                    target[n * rows + b * ROOM : n * rows + (b + 1) * ROOM, :] = got[n * ROOM : (n + 1) * ROOM]
        for n in range(local):
            for copy in fills[2 * n] + fills[2 * n + 1]:
                copy.wait()
            mine = slice(n * rows, (n + 1) * rows)
            here = dot(x_ref[mine, :], weight[:, n * hidden : (n + 1) * hidden])
            over = dot(g_ref[mine, :], weight[:, cut + n * hidden : cut + (n + 1) * hidden])
            factor = jnp.concatenate(factors[n], axis=0)
            sigmoid = jax.nn.sigmoid(here)
            act = here * sigmoid
            hid_ref[mine, :] = (factor * act).astype(BF16)
            slope_ref[mine, :] = (factor * over * (sigmoid + act * (1.0 - sigmoid))).astype(BF16)
            sums = jnp.sum(act * over, axis=1, keepdims=True)
            for b in range(count):
                hit = chosen(at_ref[b * local + n : b * local + n + 1, :], ROOM)
                spread = jnp.where(hit, sums[b * ROOM : (b + 1) * ROOM], 0.0)
                dots_ref[b * local + n : b * local + n + 1, :] = jnp.sum(spread, axis=0, keepdims=True)

    shape = lambda last, kind: jax.ShapeDtypeStruct((local * rows, last), kind)
    outs = [(NEAR, shape(width, BF16))] * 2 + [(NEAR, shape(hidden, BF16))] * 2
    outs += [(NEAR, jax.ShapeDtypeStruct((count * local, size), F32))] * 2
    return call(
        body,
        [SCALARS] + [AWAY] * (len(arrays) + len(weights)),
        outs,
        cost,
        1,
        [
            pltpu.VMEM((count, 2 * size, width), BF16),
            pltpu.VMEM((count, EXTRA, width), BF16),
            pltpu.VMEM((width, 2 * cut), BF16),
            pltpu.SemaphoreType.DMA((3 * count,)),
            pltpu.SemaphoreType.DMA((len(spans) * len(layout),)),
        ],
    )(owners, *arrays, *weights)


def outer(owners, ats, hids, slopes, dots, weights, layouts, part, parts, cost):
    ranks = len(hids)
    size = ats[0].shape[1]
    local = owners.shape[0] // ranks
    hidden = hids[0].shape[1]
    cut = local * hidden
    every = hids[0].shape[0] // local
    rows = every // parts
    blocks = rows // ROOM
    width = size * N_DP
    steps = N_ZH * N_C
    depth = width // steps
    counts = [len(some) for some in weights]
    tall = 2 * size + EXTRA

    def target(outs, b, piece):
        if b < blocks - 1:
            return outs[b], piece * size
        return (outs[b], 0) if piece == 0 else (outs[b + 1], (piece - 1) * size)

    def body(owner_ref, *refs):
        at_refs, refs = refs[:ranks], refs[ranks:]
        hid_refs, refs = refs[:ranks], refs[ranks:]
        slope_refs, refs = refs[:ranks], refs[ranks:]
        dots_refs, refs = refs[:ranks], refs[ranks:]
        flat, outs, (first, second, sem) = refs[: sum(counts)], refs[sum(counts) : -3], refs[-3:]
        sources = [flat[: counts[0]], flat[counts[0] :]]
        held = [first, second]
        fills = [[] for _ in range(steps)]
        number = 0
        for step in range(steps):
            for who in range(ranks):
                for which, start, to, many in layouts[who]:
                    if to // depth == step:
                        fills[step].append(
                            pltpu.make_async_copy(
                                sources[who][which].at[pl.ds(start, many), :],
                                held[who].at[pl.ds(to, many), :],
                                sem.at[number],
                            )
                        )
                        number += 1
        for group in fills:
            for copy in group:
                copy.start()
        picks = []
        for b in range(blocks):
            hits = []
            for who in range(ranks):
                for n in range(local):
                    row = (part * blocks + b) * local + n
                    hits.append(chosen(at_refs[who][row : row + 1, :], ROOM).astype(F32))
            picks.append(jnp.concatenate(hits, axis=0).astype(BF16))
        lines = lax.broadcasted_iota(jnp.int32, (EXTRA, size), 0)
        for b in range(blocks):
            values = []
            for who in range(ranks):
                for n in range(local):
                    row = (part * blocks + b) * local + n
                    value = dots_refs[who][row : row + 1, :]
                    high = value.astype(BF16).astype(F32)
                    values.append((owner_ref[who * local + n], high, value - high))
            for lane in range(N_DP):
                tile = jnp.zeros((EXTRA, size), F32)
                for slot, high, low in values:
                    line = jnp.where(slot % N_DP == lane, slot // N_DP, EXTRA)
                    tile = jnp.where(lines == line, high, tile)
                    tile = jnp.where(lines == line + 2, low, tile)
                out_ref, begin = target(outs, b, 2)
                out_ref[begin : begin + EXTRA, lane * size : (lane + 1) * size] = tile.astype(BF16)
        for step in range(steps):
            for copy in fills[step]:
                copy.wait()
            span = slice(step * depth, (step + 1) * depth)
            for side in (0, 1):
                made = []
                for who in range(ranks):
                    for n in range(local):
                        begin = n * every + part * rows
                        left = (hid_refs, slope_refs)[side][who][begin : begin + rows, :]
                        column = ((1 - side) * local + n) * hidden
                        made.append(dot(left, held[who][span, column : column + hidden], COLS).astype(BF16))
                for b in range(blocks):
                    stack = jnp.concatenate([m[b * ROOM : (b + 1) * ROOM] for m in made], axis=0)
                    out_ref, begin = target(outs, b, side)
                    out_ref[begin : begin + size, span] = dot(picks[b], stack, ROWS).astype(BF16)

    entries = sum(len(layout) for layout in layouts)
    return call(
        body,
        [SCALARS] + [NEAR] * (4 * ranks) + [AWAY] * sum(counts),
        [
            (NEAR, jax.ShapeDtypeStruct((many, width), BF16))
            for many in [tall] * (blocks - 1) + [size, tall - size]
        ],
        cost,
        1,
        [pltpu.VMEM((width, 2 * cut), BF16)] * 2 + [pltpu.SemaphoreType.DMA((entries,))],
    )(owners, *ats, *hids, *slopes, *dots, *[w for some in weights for w in some])


def weight_grads(toks, grds, hid, slope, local, order, cost, theirs=None):
    tall, width = toks.shape
    hidden = hid.shape[1]
    rows = tall // local
    size = width // N_DP
    group = 4
    steps = len(order) // group

    def body(*refs):
        ins, (hid_ref, slope_ref, *theirs_ref, out_ref) = refs[: 2 * group], refs[2 * group :]
        for side, other in ((0, slope_ref), (1, hid_ref)):
            these = ins[side * group : (side + 1) * group]
            for n in range(local):
                mine = slice(n * rows, (n + 1) * rows)
                left = jnp.concatenate([r[mine, :] for r in these], axis=1)
                span = slice((side * local + n) * hidden, (side * local + n + 1) * hidden)
                value = dot(left, other[mine, :], ROWS)
                for more in theirs_ref:
                    value = value + more[:, span].astype(F32)
                out_ref[:, span] = value.astype(BF16)

    def spec(n):
        places = [order[step * group + n] for step in range(steps)]

        def index(i):
            here = places[0]
            for step in range(1, steps):
                here = jnp.where(i == step, places[step], here)
            return (0, here)

        return pl.BlockSpec((tall, size), index)

    whole = pl.BlockSpec(hid.shape, lambda i: (0, 0), pipeline_mode=pl.Buffered(1))
    out = pl.BlockSpec((group * size, 2 * local * hidden), lambda i: (i, 0))
    extra = [] if theirs is None else [theirs]
    return call(
        body,
        [spec(n) for n in range(group)] * 2 + [whole, whole] + [out] * len(extra),
        [(out, jax.ShapeDtypeStruct((len(order) * size, 2 * local * hidden), BF16))],
        cost,
        1,
        (),
        (steps,),
    )(*[toks] * group, *[grds] * group, hid, slope, *extra)[0]


def per_device(tokens, grad_out, routes, probs, old_place, new_place, gate_w, gate_m, gate_v, down_w, down_m, down_v):
    tok_rows, width = tokens.shape
    experts = old_place.shape[0]
    local_count, shard, hidden = gate_w.shape
    ep, dp = lax.axis_index("ep"), lax.axis_index("dp")
    y, zl = ep // N_ZL, ep % N_ZL
    zb, za = zl // 2, zl % 2
    zh, c = dp // N_C % N_ZH, dp % N_C
    slots = jnp.arange(experts, dtype=jnp.int32)
    place = jnp.stack([zh, c]).astype(jnp.int32)

    inverse = jnp.sum(jnp.where(old_place[None, :] == slots[:, None], slots[None, :], 0), axis=1)
    slot = jnp.sum(jnp.where(routes[:, :, None] == slots, inverse, 0), axis=2)
    hits = slot.T[None] == slots[:, None, None]
    by_slot = jnp.sum(jnp.where(hits, probs.T[None], 0.0), axis=1)
    named = jnp.any(hits, axis=1)
    before = jnp.arange(tok_rows)[:, None] < jnp.arange(tok_rows)[None, :]
    number = jnp.where(named, dot(named.astype(BF16), before.astype(BF16)), -1.0)
    high = by_slot.astype(BF16)
    low = (by_slot - high.astype(F32)).astype(BF16)
    table = jnp.concatenate([number.astype(BF16), high, low], axis=0).reshape(-1, width)
    table = jnp.pad(table, ((0, EXTRA - table.shape[0]), (0, 0)))
    here = pack(place, tokens, grad_out, table)

    def side(state):
        return jnp.transpose(state, (0, 2, 1))

    weights = [gate_w, side(down_w)]
    block = jnp.concatenate([state[n] for state in weights for n in range(local_count)], axis=1)

    def gather_x(rows):
        return lax.all_gather(rows, "dp", axis=0, tiled=True, axis_index_groups=X_GROUPS)

    changed = new_place != old_place
    source = jnp.sum(jnp.where(new_place[:, None] == old_place[None, :], slots[None, :], 0), axis=1)
    first = changed & (source // local_count == (slots // local_count - 1) % N_EP)
    root = jnp.sum(jnp.where(first, slots // local_count, 0))
    mine = [jnp.any(changed & (slots == ep * local_count + n)) for n in range(local_count)]

    def migrate(payload):
        def branch(rank):
            stops = [(rank - 1) % N_EP, rank, (rank - 1 - N_EP // 2) % N_EP, (rank - 1) % N_EP]
            pairs = [(stops[0], stops[1]), (stops[2], stops[3]), (stops[1], stops[2])]
            return lambda part: lax.ppermute(part, "ep", pairs)

        return lax.switch(root, [branch(rank) for rank in range(N_EP)], payload)

    def leaving(states):
        return jnp.concatenate([jnp.where(mine[1], state[1], state[0]) for state in states], axis=1)

    states = [gate_w, gate_m, gate_v, down_w, down_m, down_v]
    payload = leaving([gate_w, gate_m, gate_v] + [side(state) for state in states[3:]])

    own_rows = gather_x(block)
    block = after(block, here)
    z_left, z_right = send(block, Z_UP), send(block, Z_DOWN)
    up, down = send(here, Y_UP), send(here, Y_DOWN)
    z_left, z_right, up, down, here, block, own_rows, payload = lax.optimization_barrier(
        (z_left, z_right, up, down, here, block, own_rows, payload)
    )
    near = jnp.concatenate([jnp.where(zb == 1, z_left, z_right), jnp.where(zb == 1, z_right, z_left)], axis=0)
    near_rows = gather_x(near)
    pair = send(here, Z_PAIR)
    far_tok, far_grd = send(up[:tok_rows], Y_UP), send(down[tok_rows:], Y_DOWN)
    pair, far_tok, far_grd, block = lax.optimization_barrier((pair, far_tok, far_grd, block))
    pair_up, pair_down = send(pair, Y_UP), send(pair, Y_DOWN)
    far = send(block, Z_FAR)
    pair_up, pair_down, far, near_rows = lax.optimization_barrier((pair_up, pair_down, far, near_rows))
    pair_far_tok, pair_far_grd = send(pair_up[:tok_rows], Y_UP), send(pair_down[tok_rows:], Y_DOWN)
    far_rows = gather_x(far)
    near_weights = [near_rows, send(near_rows, CORE)]
    own_weights = [own_rows, send(own_rows, CORE)]
    blocks = []
    for three, tok, grd in (
        ((here, up, down), far_tok, far_grd),
        ((pair, pair_up, pair_down), pair_far_tok, pair_far_grd),
    ):
        blocks += [((a, 0), (a, tok_rows)) for a in three] + [((tok, 0), (grd, 0))]
    owners = [
        jnp.stack([((y * 2 + (zb ^ who)) * 2 + za) * local_count + n for n in range(local_count)]) for who in (0, 1)
    ]

    span = N_X * shard
    own_layout = [(j * N_C + k, 0, (j * N_C + k) * span, span) for j in range(N_ZH) for k in range(N_C)]
    near_layout = [
        (k, (i * N_ZH + j) * shard, (j * N_C + k) * span + i * shard, shard)
        for j in range(N_ZH)
        for k in range(N_C)
        for i in range(N_X)
    ]

    near_x, near_g, near_hid, near_slope, near_dots, near_at = inner(
        blocks, owners[1], near_weights, near_layout, hidden, SHORT
    )

    def scatter_x(both):
        return lax.psum_scatter(both, "dp", scatter_dimension=0, tiled=True, axis_index_groups=X_GROUPS)

    def at(j, i):
        return lambda k: (j * N_C + k) * N_X + i

    order = [at(j, i) for i in range(N_X) for j in range(N_ZH)]
    theirs = weight_grads(near_x, near_g, near_hid, near_slope, local_count, [n(1) for n in order], LONG)
    theirs = send(theirs, CORE)
    ours = weight_grads(near_x, near_g, near_hid, near_slope, local_count, [n(0) for n in order], LONG)
    near_sum = add(ours, theirs)

    payload = after(payload, near_hid)
    across, following = send_ep(payload, E_HALF), send_ep(payload, E_NEXT)
    far_rows, owners[0], near_sum, across = lax.optimization_barrier((far_rows, owners[0], near_sum, across))
    arrivals = [following, across, send_ep(across, E_PREV)]
    own_weights += [far_rows, send(far_rows, CORE)]
    near_grads = scatter_x(near_sum)
    own_x, own_g, own_hid, own_slope, own_dots, own_at = inner(
        blocks, owners[0], own_weights, own_layout, hidden, 1
    )
    theirs = weight_grads(own_x, own_g, own_hid, own_slope, local_count, [n(1) for n in order], 1)

    owners = jnp.concatenate(owners)

    def made(part, cost, *others):
        return outer(
            after(owners, *others),
            [own_at, near_at],
            [own_hid, near_hid],
            [own_slope, near_slope],
            [own_dots, near_dots],
            [own_weights, near_weights],
            [own_layout, near_layout],
            part,
            2,
            cost,
        )

    def halves(far_tok, far_rest):
        return send(far_tok, Y_UP), send(far_rest, Y_DOWN)

    mine_late, left, right, *far = made(1, LONG, theirs, arrivals[2])
    far_late = halves(*far)
    own_sum = weight_grads(
        after(own_x, left, following),
        own_g,
        own_hid,
        own_slope,
        local_count,
        [n(0) for n in order],
        LONG,
        send(theirs, CORE),
    )
    own_sum, near_grads, far_late, left, right = lax.optimization_barrier(
        (own_sum, near_grads, far_late, left, right)
    )
    own_grads = scatter_x(own_sum)
    left, right = passed(left, right, *far_late)
    late = [mine_late, send(right, Y_UP), send(left, Y_DOWN)]
    near_grads = [near_grads[:shard], near_grads[shard:]]
    to_right = jnp.where(zb == 1, near_grads[1], near_grads[0])
    to_left = jnp.where(zb == 1, near_grads[0], near_grads[1])
    from_z = [send(to_right, Z_UP), send(to_left, Z_DOWN)]
    mine_soon, next_left, next_right, *next_far = made(0, LONG, own_sum, left, right, to_right, to_left)
    next_far, from_z, place = lax.optimization_barrier((next_far, from_z, place))
    far_soon = halves(*next_far)
    late, place = lax.optimization_barrier((late, hold(place)))
    other = functools.reduce(lambda a, b: a + b, [p.astype(F32) for p in late]).astype(BF16)
    far_soon, place = lax.optimization_barrier((far_soon, hold(after(place, other))))
    left, right = passed(next_left, next_right, *far_soon)
    soon = [mine_soon, send(right, Y_UP), send(left, Y_DOWN)]
    own_grads, place = lax.optimization_barrier((own_grads, hold(after(place, left, right))))
    terms = [own_grads[:shard], *from_z, send(own_grads[shard:], Z_FAR)]
    grad = functools.reduce(lambda a, b: a + b, [term.astype(F32) for term in terms])
    grad, place = lax.optimization_barrier((grad, place))
    mixed, grad_tokens, table = total(place, *soon, send(other, Z_PAIR))
    table = table[: 2 * experts // N_DP].reshape(2, experts, tok_rows)
    grad_probs = jnp.sum(jnp.where(hits, (table[0] + table[1])[:, None, :], 0.0), axis=0).T

    grads = [[grad[:, (s * local_count + n) * hidden :][:, :hidden] for n in range(local_count)] for s in (0, 1)]
    moved = migrate(leaving(grads).astype(BF16))
    arrived = jnp.where(ep == root, arrivals[0], jnp.where(ep == (root - 1) % N_EP, arrivals[1], arrivals[2]))
    mine = jnp.stack(mine).astype(jnp.int32)
    return (mixed, grad_tokens, grad_probs, *updates(mine, grad, moved, states, arrived))


def solution(mesh):
    tok = P(("ep", "dp"), None)
    gate, down = P("ep", "dp", None), P("ep", None, "dp")
    in_specs = (tok, tok, tok, tok, P(), P(), gate, gate, gate, down, down, down)
    out_specs = (tok, tok, tok, gate, gate, gate, down, down, down)
    return jax.shard_map(per_device, mesh=mesh, in_specs=in_specs, out_specs=out_specs, check_vma=False)
```

```python
import functools
import jax
import jax.numpy as jnp
from jax import lax
from jax.experimental import pallas as pl
from jax.experimental.pallas import tpu as pltpu
from jax.sharding import PartitionSpec as P

beta_one = 0.9
beta_two = 0.95
step_rate = 0.001
adam_eps = 1e-08

BOTH = ("ep", "dp")
N_Y, N_ZL, N_X, N_ZH, N_C = 4, 4, 4, 2, 2
N_EP, N_DP = N_Y * N_ZL, N_X * N_ZH * N_C
F32, BF16 = jnp.float32, jnp.bfloat16


def links(move):
    pairs = []
    for ep in range(N_EP):
        for dp in range(N_DP):
            y, zl = divmod(ep, N_ZL)
            x, rest = divmod(dp, N_ZH * N_C)
            zh, c = divmod(rest, N_C)
            y, x, z, c = move(y, x, zh * N_ZL + zl, c)
            zh, zl = divmod(z % (N_ZH * N_ZL), N_ZL)
            there = (y % N_Y * N_ZL + zl) * N_DP + x % N_X * N_ZH * N_C + zh * N_C + c
            pairs.append((ep * N_DP + dp, there))
    return pairs


Y_UP = links(lambda y, x, z, c: (y + 1, x, z, c))
Y_DOWN = links(lambda y, x, z, c: (y - 1, x, z, c))
X_UP = links(lambda y, x, z, c: (y, x + 1, z, c))
X_DOWN = links(lambda y, x, z, c: (y, x - 1, z, c))
Z_UP = links(lambda y, x, z, c: (y, x, z + 2, c))
Z_DOWN = links(lambda y, x, z, c: (y, x, z - 2, c))
Z_PAIR = links(lambda y, x, z, c: (y, x, z ^ 1, c))
Z_FAR = links(lambda y, x, z, c: (y, x, z + 4, c))
X_GROUPS = [[i * N_ZH * N_C + rest for i in range(N_X)] for rest in range(N_ZH * N_C)]
ROOM = 48
EXTRA = 16
VMEM = 56 * 2**20
SHORT, LONG = 10**9, 10**12
CORE = links(lambda y, x, z, c: (y, x, z, 1 - c))


E_NEXT = [(rank, (rank + 1) % N_EP) for rank in range(N_EP)]
E_HALF = [(rank, (rank + N_EP // 2) % N_EP) for rank in range(N_EP)]
E_PREV = [(rank, (rank - 1) % N_EP) for rank in range(N_EP)]


def after(array, *others):
    return lax.optimization_barrier((array, *others))[0]


def send(block, pairs):
    return lax.ppermute(block, BOTH, pairs)


def send_ep(block, pairs):
    return lax.ppermute(block, "ep", pairs)


def add(first, second):
    return (first.astype(F32) + second.astype(F32)).astype(BF16)


def adam_update(weight, first, second, grad):
    first_new = beta_one * first.astype(F32) + (1.0 - beta_one) * grad
    second_new = beta_two * second.astype(F32) + (1.0 - beta_two) * grad * grad
    weight_new = weight.astype(F32) - step_rate * first_new / (jnp.sqrt(second_new) + adam_eps)
    return weight_new.astype(BF16), first_new.astype(BF16), second_new.astype(BF16)


def updates(mine, grad, moved, states, arrived):
    local, shard, hidden = states[0].shape

    def body(mine_ref, grad_ref, moved_ref, *refs):
        ins, arrived_ref, outs = refs[:6], refs[6], refs[7:]
        for n in range(local):
            here = mine_ref[n] > 0
            for side in (0, 1):
                span = slice((side * local + n) * hidden, (side * local + n + 1) * hidden)
                value = jnp.where(here, moved_ref[:, side * hidden : (side + 1) * hidden].astype(F32), grad_ref[:, span])
                if side:
                    value = value.T
                state = []
                for kind in range(3):
                    column = (side * 3 + kind) * hidden
                    fresh = arrived_ref[:, column : column + hidden].astype(F32)
                    old = ins[side * 3 + kind][n].astype(F32)
                    state.append(jnp.where(here, fresh.T if side else fresh, old))
                for kind, done in enumerate(adam_update(*state, value)):
                    outs[side * 3 + kind][n] = done

    shapes = [jax.ShapeDtypeStruct(state.shape, BF16) for state in states]
    moved_bytes = 4 * 6 * local * shard * hidden
    return call(
        body, [SCALARS] + [NEAR] * 9, [(NEAR, shape) for shape in shapes], 0, moved_bytes
    )(mine, grad, moved, *states, arrived)


def dot(left, right, dims=((1,), (0,))):
    return lax.dot_general(left, right, (dims, ((), ())), preferred_element_type=F32)


COLS = ((1,), (1,))
ROWS = ((0,), (0,))
NEAR = pl.BlockSpec(memory_space=pltpu.VMEM)
AWAY = pl.BlockSpec(memory_space=pl.ANY)
SCALARS = pl.BlockSpec(memory_space=pltpu.SMEM)


def call(body, ins, outs, flops, moved, scratch=(), grid=()):
    return pl.pallas_call(
        body,
        grid=grid,
        in_specs=list(ins),
        out_specs=[spec for spec, _ in outs],
        out_shape=[shape for _, shape in outs],
        scratch_shapes=list(scratch),
        compiler_params=pltpu.CompilerParams(vmem_limit_bytes=VMEM),
        cost_estimate=pl.CostEstimate(flops=flops, bytes_accessed=moved, transcendentals=0),
    )


def relative(n, zh, c):
    j, k, i = n // (N_C * N_X), n // N_X % N_C, n % N_X
    return (i * N_ZH + (j ^ zh)) * N_C + (k ^ c)


def pack(place, tokens, grads, table):
    rows, width = tokens.shape
    block = width // N_DP

    def body(place_ref, tok_ref, grd_ref, table_ref, out_ref):
        zh, c = place_ref[0], place_ref[1]
        for n in range(N_DP):
            at = pl.multiple_of(relative(n, zh, c) * block, block)
            here = slice(n * block, (n + 1) * block)
            out_ref[:rows, here] = tok_ref[:, pl.ds(at, block)]
            out_ref[rows : 2 * rows, here] = grd_ref[:, pl.ds(at, block)]
        out_ref[2 * rows :, :] = table_ref[...]

    shape = jax.ShapeDtypeStruct((2 * rows + EXTRA, width), BF16)
    return call(body, [SCALARS] + [NEAR] * 3, [(NEAR, shape)], 0, 8 * rows * width)(place, tokens, grads, table)[0]


def total(place, *arrays):
    rows, width = arrays[0].shape
    rows = (rows - EXTRA) // 2
    block = width // N_DP

    def body(place_ref, *refs):
        zh, c = place_ref[0], place_ref[1]
        ins, (mixed_ref, back_ref, table_ref) = refs[:-3], refs[-3:]

        def added(at, here):
            value = ins[0][at, here].astype(F32)
            for source in ins[1:]:
                value = value + source[at, here].astype(F32)
            return value

        for n in range(N_DP):
            at = pl.multiple_of(relative(n, zh, c) * block, block)
            here = slice(n * block, (n + 1) * block)
            mixed_ref[:, pl.ds(at, block)] = added(slice(0, rows), here).astype(BF16)
            back_ref[:, pl.ds(at, block)] = added(slice(rows, 2 * rows), here).astype(BF16)
        table_ref[...] = added(slice(2 * rows, 2 * rows + EXTRA), slice(0, width))

    outs = [(NEAR, jax.ShapeDtypeStruct((rows, width), BF16))] * 2
    outs.append((NEAR, jax.ShapeDtypeStruct((EXTRA, width), F32)))
    return call(body, [SCALARS] + [NEAR] * len(arrays), outs, 0, 20 * rows * width)(place, *arrays)


def hold(place):
    def body(place_ref, out_ref):
        for n in range(2):
            out_ref[n] = place_ref[n]

    return call(body, [SCALARS], [(SCALARS, jax.ShapeDtypeStruct(place.shape, place.dtype))], 2**40, 0)(place)[0]


def passed(left, right, from_left, from_right):
    size = from_left.shape[0]
    width = left.shape[1]

    def body(left_ref, right_ref, from_left_ref, from_right_ref, left_out, right_out):
        left_out[:size] = left_ref[:size]
        left_out[size:] = add(left_ref[size:], from_right_ref[...])
        right_out[:size] = add(right_ref[:size], from_left_ref[...])
        right_out[size:] = right_ref[size:]

    tile = width // 4
    down = lambda array: pl.BlockSpec((array.shape[0], tile), lambda i: (0, i))
    arrays = (left, right, from_left, from_right)
    shape = jax.ShapeDtypeStruct(left.shape, BF16)
    return call(body, [down(a) for a in arrays], [(down(left), shape)] * 2, 0, 0, (), (4,))(*arrays)


def chosen(at, rows):
    return lax.broadcasted_iota(jnp.int32, (rows, at.shape[1]), 0).astype(F32) == at


def inner(blocks, owners, weights, layout, hidden, cost):
    count = len(blocks)
    size, width = blocks[0][0][0].shape[1] // N_DP, blocks[0][0][0].shape[1]
    local = owners.shape[0]
    cut = local * hidden
    rows = count * ROOM
    arrays = []
    for block in blocks:
        for array, _ in block:
            if not any(array is other for other in arrays):
                arrays.append(array)
    index = lambda array: next(n for n, other in enumerate(arrays) if other is array)
    starts = [[(index(array), start) for array, start in block] for block in blocks]
    spans = [(side * local + n) * hidden for n in range(local) for side in (0, 1)]

    def body(owner_ref, *refs):
        sources, stored = refs[: len(arrays)], refs[len(arrays) : len(arrays) + len(weights)]
        x_ref, g_ref, hid_ref, slope_ref, dots_ref, at_ref, held, tables, weight, sem, weight_sem = refs[
            len(arrays) + len(weights) :
        ]
        moves, fills = [], []
        for b, block in enumerate(starts):
            moves.append(
                [
                    pltpu.make_async_copy(
                        sources[which].at[pl.ds(start, size), :],
                        held.at[b, pl.ds(side * size, size), :],
                        sem.at[2 * b + side],
                    )
                    for side, (which, start) in enumerate(block)
                ]
            )
            which, start = block[1]
            moves[b].append(
                pltpu.make_async_copy(
                    sources[which].at[pl.ds(start + size, EXTRA), :], tables.at[b], sem.at[2 * count + b]
                )
            )
        for number, span in enumerate(spans):
            fills.append(
                [
                    pltpu.make_async_copy(
                        stored[which].at[pl.ds(start, depth), pl.ds(span, hidden)],
                        weight.at[pl.ds(to, depth), pl.ds(span, hidden)],
                        weight_sem.at[number * len(layout) + entry],
                    )
                    for entry, (which, start, to, depth) in enumerate(layout)
                ]
            )
        for group in moves + fills:
            for copy in group:
                copy.start()
        factors = [[] for _ in range(local)]
        lines = lax.broadcasted_iota(jnp.int32, (EXTRA, size), 0)
        for b in range(count):
            for copy in moves[b]:
                copy.wait()
            hits = []
            for n in range(local):
                slot = owner_ref[n]
                lanes = pl.ds(pl.multiple_of(slot % N_DP * size, size), size)
                tile = tables[b, :, lanes].astype(F32)
                line = slot // N_DP
                entry = lambda kind: jnp.sum(jnp.where(lines == line + 2 * kind, tile, 0.0), axis=0, keepdims=True)
                number = entry(0)
                at_ref[b * local + n : b * local + n + 1, :] = number
                hits.append(chosen(number, ROOM))
                factors[n].append(jnp.sum(jnp.where(hits[n], entry(1) + entry(2), 0.0), axis=1, keepdims=True))
            pick = jnp.concatenate([hit.astype(F32) for hit in hits], axis=0).astype(BF16)
            for side, target in enumerate((x_ref, g_ref)):
                got = dot(pick, held[b, side * size : (side + 1) * size, :]).astype(BF16)
                for n in range(local):
                    target[n * rows + b * ROOM : n * rows + (b + 1) * ROOM, :] = got[n * ROOM : (n + 1) * ROOM]
        for n in range(local):
            for copy in fills[2 * n] + fills[2 * n + 1]:
                copy.wait()
            mine = slice(n * rows, (n + 1) * rows)
            here = dot(x_ref[mine, :], weight[:, n * hidden : (n + 1) * hidden])
            over = dot(g_ref[mine, :], weight[:, cut + n * hidden : cut + (n + 1) * hidden])
            factor = jnp.concatenate(factors[n], axis=0)
            sigmoid = jax.nn.sigmoid(here)
            act = here * sigmoid
            hid_ref[mine, :] = (factor * act).astype(BF16)
            slope_ref[mine, :] = (factor * over * (sigmoid + act * (1.0 - sigmoid))).astype(BF16)
            sums = jnp.sum(act * over, axis=1, keepdims=True)
            for b in range(count):
                hit = chosen(at_ref[b * local + n : b * local + n + 1, :], ROOM)
                spread = jnp.where(hit, sums[b * ROOM : (b + 1) * ROOM], 0.0)
                dots_ref[b * local + n : b * local + n + 1, :] = jnp.sum(spread, axis=0, keepdims=True)

    shape = lambda last, kind: jax.ShapeDtypeStruct((local * rows, last), kind)
    outs = [(NEAR, shape(width, BF16))] * 2 + [(NEAR, shape(hidden, BF16))] * 2
    outs += [(NEAR, jax.ShapeDtypeStruct((count * local, size), F32))] * 2
    return call(
        body,
        [SCALARS] + [AWAY] * (len(arrays) + len(weights)),
        outs,
        cost,
        1,
        [
            pltpu.VMEM((count, 2 * size, width), BF16),
            pltpu.VMEM((count, EXTRA, width), BF16),
            pltpu.VMEM((width, 2 * cut), BF16),
            pltpu.SemaphoreType.DMA((3 * count,)),
            pltpu.SemaphoreType.DMA((len(spans) * len(layout),)),
        ],
    )(owners, *arrays, *weights)


def outer(owners, ats, hids, slopes, dots, weights, layouts, part, parts, cost):
    ranks = len(hids)
    size = ats[0].shape[1]
    local = owners.shape[0] // ranks
    hidden = hids[0].shape[1]
    cut = local * hidden
    every = hids[0].shape[0] // local
    rows = every // parts
    blocks = rows // ROOM
    width = size * N_DP
    steps = N_ZH * N_C
    depth = width // steps
    counts = [len(some) for some in weights]
    tall = 2 * size + EXTRA

    def target(outs, b, piece):
        if b < blocks - 1:
            return outs[b], piece * size
        return (outs[b], 0) if piece == 0 else (outs[b + 1], (piece - 1) * size)

    def body(owner_ref, *refs):
        at_refs, refs = refs[:ranks], refs[ranks:]
        hid_refs, refs = refs[:ranks], refs[ranks:]
        slope_refs, refs = refs[:ranks], refs[ranks:]
        dots_refs, refs = refs[:ranks], refs[ranks:]
        flat, outs, (first, second, sem) = refs[: sum(counts)], refs[sum(counts) : -3], refs[-3:]
        sources = [flat[: counts[0]], flat[counts[0] :]]
        held = [first, second]
        fills = [[] for _ in range(steps)]
        number = 0
        for step in range(steps):
            for who in range(ranks):
                for which, start, to, many in layouts[who]:
                    if to // depth == step:
                        fills[step].append(
                            pltpu.make_async_copy(
                                sources[who][which].at[pl.ds(start, many), :],
                                held[who].at[pl.ds(to, many), :],
                                sem.at[number],
                            )
                        )
                        number += 1
        for group in fills:
            for copy in group:
                copy.start()
        picks = []
        for b in range(blocks):
            hits = []
            for who in range(ranks):
                for n in range(local):
                    row = (part * blocks + b) * local + n
                    hits.append(chosen(at_refs[who][row : row + 1, :], ROOM).astype(F32))
            picks.append(jnp.concatenate(hits, axis=0).astype(BF16))
        lines = lax.broadcasted_iota(jnp.int32, (EXTRA, size), 0)
        for b in range(blocks):
            values = []
            for who in range(ranks):
                for n in range(local):
                    row = (part * blocks + b) * local + n
                    value = dots_refs[who][row : row + 1, :]
                    high = value.astype(BF16).astype(F32)
                    values.append((owner_ref[who * local + n], high, value - high))
            for lane in range(N_DP):
                tile = jnp.zeros((EXTRA, size), F32)
                for slot, high, low in values:
                    line = jnp.where(slot % N_DP == lane, slot // N_DP, EXTRA)
                    tile = jnp.where(lines == line, high, tile)
                    tile = jnp.where(lines == line + 2, low, tile)
                out_ref, begin = target(outs, b, 2)
                out_ref[begin : begin + EXTRA, lane * size : (lane + 1) * size] = tile.astype(BF16)
        for step in range(steps):
            for copy in fills[step]:
                copy.wait()
            span = slice(step * depth, (step + 1) * depth)
            for side in (0, 1):
                made = []
                for who in range(ranks):
                    for n in range(local):
                        begin = n * every + part * rows
                        left = (hid_refs, slope_refs)[side][who][begin : begin + rows, :]
                        column = ((1 - side) * local + n) * hidden
                        made.append(dot(left, held[who][span, column : column + hidden], COLS).astype(BF16))
                for b in range(blocks):
                    stack = jnp.concatenate([m[b * ROOM : (b + 1) * ROOM] for m in made], axis=0)
                    out_ref, begin = target(outs, b, side)
                    out_ref[begin : begin + size, span] = dot(picks[b], stack, ROWS).astype(BF16)

    entries = sum(len(layout) for layout in layouts)
    return call(
        body,
        [SCALARS] + [NEAR] * (4 * ranks) + [AWAY] * sum(counts),
        [
            (NEAR, jax.ShapeDtypeStruct((many, width), BF16))
            for many in [tall] * (blocks - 1) + [size, tall - size]
        ],
        cost,
        1,
        [pltpu.VMEM((width, 2 * cut), BF16)] * 2 + [pltpu.SemaphoreType.DMA((entries,))],
    )(owners, *ats, *hids, *slopes, *dots, *[w for some in weights for w in some])


def weight_grads(toks, grds, hid, slope, local, order, cost, theirs=None):
    tall, width = toks.shape
    hidden = hid.shape[1]
    rows = tall // local
    size = width // N_DP
    group = 2
    steps = len(order) // group

    def body(*refs):
        ins, (hid_ref, slope_ref, *theirs_ref, out_ref) = refs[: 2 * group], refs[2 * group :]
        for side, other in ((0, slope_ref), (1, hid_ref)):
            these = ins[side * group : (side + 1) * group]
            for n in range(local):
                mine = slice(n * rows, (n + 1) * rows)
                left = jnp.concatenate([r[mine, :] for r in these], axis=1)
                span = slice((side * local + n) * hidden, (side * local + n + 1) * hidden)
                value = dot(left, other[mine, :], ROWS)
                for more in theirs_ref:
                    value = value + more[:, span].astype(F32)
                out_ref[:, span] = value.astype(BF16)

    def spec(n):
        places = [order[step * group + n] for step in range(steps)]

        def index(i):
            here = places[0]
            for step in range(1, steps):
                here = jnp.where(i == step, places[step], here)
            return (0, here)

        return pl.BlockSpec((tall, size), index)

    whole = pl.BlockSpec(hid.shape, lambda i: (0, 0), pipeline_mode=pl.Buffered(1))
    out = pl.BlockSpec((group * size, 2 * local * hidden), lambda i: (i, 0))
    extra = [] if theirs is None else [theirs]
    return call(
        body,
        [spec(n) for n in range(group)] * 2 + [whole, whole] + [out] * len(extra),
        [(out, jax.ShapeDtypeStruct((len(order) * size, 2 * local * hidden), BF16))],
        cost,
        1,
        (),
        (steps,),
    )(*[toks] * group, *[grds] * group, hid, slope, *extra)[0]


def per_device(tokens, grad_out, routes, probs, old_place, new_place, gate_w, gate_m, gate_v, down_w, down_m, down_v):
    tok_rows, width = tokens.shape
    experts = old_place.shape[0]
    local_count, shard, hidden = gate_w.shape
    ep, dp = lax.axis_index("ep"), lax.axis_index("dp")
    y, zl = ep // N_ZL, ep % N_ZL
    zb, za = zl // 2, zl % 2
    zh, c = dp // N_C % N_ZH, dp % N_C
    slots = jnp.arange(experts, dtype=jnp.int32)
    place = jnp.stack([zh, c]).astype(jnp.int32)

    inverse = jnp.sum(jnp.where(old_place[None, :] == slots[:, None], slots[None, :], 0), axis=1)
    slot = jnp.sum(jnp.where(routes[:, :, None] == slots, inverse, 0), axis=2)
    hits = slot.T[None] == slots[:, None, None]
    by_slot = jnp.sum(jnp.where(hits, probs.T[None], 0.0), axis=1)
    named = jnp.any(hits, axis=1)
    before = jnp.arange(tok_rows)[:, None] < jnp.arange(tok_rows)[None, :]
    number = jnp.where(named, dot(named.astype(BF16), before.astype(BF16)), -1.0)
    high = by_slot.astype(BF16)
    low = (by_slot - high.astype(F32)).astype(BF16)
    table = jnp.concatenate([number.astype(BF16), high, low], axis=0).reshape(-1, width)
    table = jnp.pad(table, ((0, EXTRA - table.shape[0]), (0, 0)))
    here = pack(place, tokens, grad_out, table)

    def side(state):
        return jnp.transpose(state, (0, 2, 1))

    weights = [gate_w, side(down_w)]
    block = jnp.concatenate([state[n] for state in weights for n in range(local_count)], axis=1)

    def gather_x(rows):
        return lax.all_gather(rows, "dp", axis=0, tiled=True, axis_index_groups=X_GROUPS)

    changed = new_place != old_place
    source = jnp.sum(jnp.where(new_place[:, None] == old_place[None, :], slots[None, :], 0), axis=1)
    first = changed & (source // local_count == (slots // local_count - 1) % N_EP)
    root = jnp.sum(jnp.where(first, slots // local_count, 0))
    mine = [jnp.any(changed & (slots == ep * local_count + n)) for n in range(local_count)]

    def migrate(payload):
        def branch(rank):
            stops = [(rank - 1) % N_EP, rank, (rank - 1 - N_EP // 2) % N_EP, (rank - 1) % N_EP]
            pairs = [(stops[0], stops[1]), (stops[2], stops[3]), (stops[1], stops[2])]
            return lambda part: lax.ppermute(part, "ep", pairs)

        return lax.switch(root, [branch(rank) for rank in range(N_EP)], payload)

    def leaving(states):
        return jnp.concatenate([jnp.where(mine[1], state[1], state[0]) for state in states], axis=1)

    states = [gate_w, gate_m, gate_v, down_w, down_m, down_v]
    payload = leaving([gate_w, gate_m, gate_v] + [side(state) for state in states[3:]])

    own_rows = gather_x(block)
    block = after(block, here)
    z_left, z_right = send(block, Z_UP), send(block, Z_DOWN)
    up, down = send(here, Y_UP), send(here, Y_DOWN)
    z_left, z_right, up, down, here, block, own_rows, payload = lax.optimization_barrier(
        (z_left, z_right, up, down, here, block, own_rows, payload)
    )
    near = jnp.concatenate([jnp.where(zb == 1, z_left, z_right), jnp.where(zb == 1, z_right, z_left)], axis=0)
    near_rows = gather_x(near)
    pair = send(here, Z_PAIR)
    far_tok, far_grd = send(up[:tok_rows], Y_UP), send(down[tok_rows:], Y_DOWN)
    pair, far_tok, far_grd, block = lax.optimization_barrier((pair, far_tok, far_grd, block))
    pair_up, pair_down = send(pair, Y_UP), send(pair, Y_DOWN)
    far = send(block, Z_FAR)
    pair_up, pair_down, far, near_rows = lax.optimization_barrier((pair_up, pair_down, far, near_rows))
    pair_far_tok, pair_far_grd = send(pair_up[:tok_rows], Y_UP), send(pair_down[tok_rows:], Y_DOWN)
    far_rows = gather_x(far)
    near_weights = [near_rows, send(near_rows, CORE)]
    own_weights = [own_rows, send(own_rows, CORE)]
    blocks = []
    for three, tok, grd in (
        ((here, up, down), far_tok, far_grd),
        ((pair, pair_up, pair_down), pair_far_tok, pair_far_grd),
    ):
        blocks += [((a, 0), (a, tok_rows)) for a in three] + [((tok, 0), (grd, 0))]
    owners = [
        jnp.stack([((y * 2 + (zb ^ who)) * 2 + za) * local_count + n for n in range(local_count)]) for who in (0, 1)
    ]

    span = N_X * shard
    own_layout = [(j * N_C + k, 0, (j * N_C + k) * span, span) for j in range(N_ZH) for k in range(N_C)]
    near_layout = [
        (k, (i * N_ZH + j) * shard, (j * N_C + k) * span + i * shard, shard)
        for j in range(N_ZH)
        for k in range(N_C)
        for i in range(N_X)
    ]

    near_x, near_g, near_hid, near_slope, near_dots, near_at = inner(
        blocks, owners[1], near_weights, near_layout, hidden, SHORT
    )

    def scatter_x(both):
        return lax.psum_scatter(both, "dp", scatter_dimension=0, tiled=True, axis_index_groups=X_GROUPS)

    def at(j, i):
        return lambda k: (j * N_C + k) * N_X + i

    order = [at(j, i) for i in range(N_X) for j in range(N_ZH)]
    theirs = weight_grads(near_x, near_g, near_hid, near_slope, local_count, [n(1) for n in order], LONG)
    theirs = send(theirs, CORE)
    ours = weight_grads(near_x, near_g, near_hid, near_slope, local_count, [n(0) for n in order], LONG)
    near_sum = add(ours, theirs)

    payload = after(payload, near_hid)
    across, following = send_ep(payload, E_HALF), send_ep(payload, E_NEXT)
    far_rows, owners[0], near_sum, across = lax.optimization_barrier((far_rows, owners[0], near_sum, across))
    arrivals = [following, across, send_ep(across, E_PREV)]
    own_weights += [far_rows, send(far_rows, CORE)]
    near_grads = scatter_x(near_sum)
    own_x, own_g, own_hid, own_slope, own_dots, own_at = inner(
        blocks, owners[0], own_weights, own_layout, hidden, 1
    )
    theirs = weight_grads(own_x, own_g, own_hid, own_slope, local_count, [n(1) for n in order], 1)

    owners = jnp.concatenate(owners)

    def made(part, cost, *others):
        return outer(
            after(owners, *others),
            [own_at, near_at],
            [own_hid, near_hid],
            [own_slope, near_slope],
            [own_dots, near_dots],
            [own_weights, near_weights],
            [own_layout, near_layout],
            part,
            2,
            cost,
        )

    def halves(far_tok, far_rest):
        return send(far_tok, Y_UP), send(far_rest, Y_DOWN)

    mine_late, left, right, *far = made(1, LONG, theirs, arrivals[2])
    far_late = halves(*far)
    own_sum = weight_grads(
        after(own_x, left, following),
        own_g,
        own_hid,
        own_slope,
        local_count,
        [n(0) for n in order],
        LONG,
        send(theirs, CORE),
    )
    own_sum, near_grads, far_late, left, right = lax.optimization_barrier(
        (own_sum, near_grads, far_late, left, right)
    )
    own_grads = scatter_x(own_sum)
    left, right = passed(left, right, *far_late)
    late = [mine_late, send(right, Y_UP), send(left, Y_DOWN)]
    near_grads = [near_grads[:shard], near_grads[shard:]]
    to_right = jnp.where(zb == 1, near_grads[1], near_grads[0])
    to_left = jnp.where(zb == 1, near_grads[0], near_grads[1])
    from_z = [send(to_right, Z_UP), send(to_left, Z_DOWN)]
    mine_soon, next_left, next_right, *next_far = made(0, LONG, own_sum, left, right, to_right, to_left)
    next_far, from_z, place = lax.optimization_barrier((next_far, from_z, place))
    far_soon = halves(*next_far)
    late, place = lax.optimization_barrier((late, hold(place)))
    other = functools.reduce(lambda a, b: a + b, [p.astype(F32) for p in late]).astype(BF16)
    far_soon, place = lax.optimization_barrier((far_soon, hold(after(place, other))))
    left, right = passed(next_left, next_right, *far_soon)
    soon = [mine_soon, send(right, Y_UP), send(left, Y_DOWN)]
    own_grads, place = lax.optimization_barrier((own_grads, hold(after(place, left, right))))
    terms = [own_grads[:shard], *from_z, send(own_grads[shard:], Z_FAR)]
    grad = functools.reduce(lambda a, b: a + b, [term.astype(F32) for term in terms])
    grad, place = lax.optimization_barrier((grad, place))
    mixed, grad_tokens, table = total(place, *soon, send(other, Z_PAIR))
    table = table[: 2 * experts // N_DP].reshape(2, experts, tok_rows)
    grad_probs = jnp.sum(jnp.where(hits, (table[0] + table[1])[:, None, :], 0.0), axis=0).T

    grads = [[grad[:, (s * local_count + n) * hidden :][:, :hidden] for n in range(local_count)] for s in (0, 1)]
    moved = migrate(leaving(grads).astype(BF16))
    arrived = jnp.where(ep == root, arrivals[0], jnp.where(ep == (root - 1) % N_EP, arrivals[1], arrivals[2]))
    mine = jnp.stack(mine).astype(jnp.int32)
    return (mixed, grad_tokens, grad_probs, *updates(mine, grad, moved, states, arrived))


def solution(mesh):
    tok = P(("ep", "dp"), None)
    gate, down = P("ep", "dp", None), P("ep", None, "dp")
    in_specs = (tok, tok, tok, tok, P(), P(), gate, gate, gate, down, down, down)
    out_specs = (tok, tok, tok, gate, gate, gate, down, down, down)
    return jax.shard_map(per_device, mesh=mesh, in_specs=in_specs, out_specs=out_specs, check_vma=False)
```
